256 devices in a mesh: grp: 8 (over z_lo, x), dev: 32 (over z_hi, y, core).
Axes of the slice: x: 4, y: 4, z: 8 (z_hi: 4, z_lo: 2; z = z_hi * 2 + z_lo), core: 2. Of those that a mesh axis runs over, the one named last changes fastest.
Arguments:
- velocity: float32 [3, 256, 64, 1024], P(None, 'dev', None, 'grp'), may hold values from -5 to 5
- viscosity: float32 [256, 64, 1024], P('dev', None, 'grp'), may hold values from 0.2 to 2
- positions: float32 [3, 32768], P(None, ('grp', 'dev')), may hold values from -16 to 16
- weights: bfloat16 [32768, 128], P(('grp', 'dev')), may hold values from 0 to 0.049804688
- tile_index: int32 [32768], P(('grp', 'dev')), may hold values from 0 to 16383, as said below
- links: int32 [32768, 2], P(('grp', 'dev')), may hold values from 0 to 4095
Outputs:
- new_velocity: float32 [3, 256, 64, 1024], P(None, 'dev', None, 'grp')
- moved: float32 [3, 32768], P(None, ('grp', 'dev'))
- point_force: float32 [3, 32768], P(None, ('grp', 'dev'))
The draws below stay inside these ranges and needn't reach their ends.
Inputs may be any that keep to these rules, and one draw needn't show every extreme that they name: `tile_index`: among the 128 points of one device (an aligned block of rows), at most 16 have tiles t with the same t // 512; in each group one value of t // 512 is taken by exactly 16 points of every device of the group.
All inputs are finite; a program needn't handle non-finite values.
Results may differ from the reference program's by a relative error of at most 0.0019.
Values may be sent and summed in bfloat16 or wider, within the bound.
No kernel may reach another device: no remote copies, remote signals or barrier semaphores. Data moves between devices by JAX's collectives and lax.ppermute only.
A program may use at most 128 MiB of HBM per device.

```python
import math
import jax
import jax.numpy as jnp
import numpy as np

NY = 64
CZ = 128
P_DEV = 128
NX = 256
NZ = 1024
P_GRP = 4096
P_TOTAL = 32768
TILES_DEV = 512
TILES_SLAB = 16384
N_GRP = 8
N_DEV = 32


def shuffle_one(perm_key):
    return jax.random.permutation(perm_key, P_DEV)


def draw_tile_index(key, part):
    key = jax.random.fold_in(key, 7)
    hottest_key, shuffle_key, cell_key = jax.random.split(key, 3)
    capacity = 4 * P_DEV // N_DEV
    leftover = P_DEV - capacity
    spread_base = leftover // (N_DEV - 1)
    remainder = leftover % (N_DEV - 1)
    load_list = [capacity] + [spread_base + (1 if step < remainder else 0) for step in range(N_DEV - 1)]
    offset_table = jnp.asarray(np.repeat(np.arange(N_DEV), load_list).astype(np.int32))
    hottest = jax.random.randint(hottest_key, (N_GRP, 1, 1), 0, N_DEV)
    shuffle_keys = jax.random.split(shuffle_key, N_GRP * N_DEV)
    shuffled = jax.vmap(shuffle_one)(shuffle_keys).reshape(N_GRP, N_DEV, P_DEV)
    owners = (hottest + offset_table[shuffled]) % N_DEV
    cells_in = jax.random.randint(cell_key, (N_GRP, N_DEV, P_DEV), 0, TILES_DEV)
    return (owners * TILES_DEV + cells_in).reshape(P_TOTAL).astype(jnp.int32)


def phase_along(cycles, length):
    index_line = jnp.arange(length, dtype=jnp.int32)
    return (cycles[:, None] * index_line[None, :] % length).astype(jnp.float32) / length


def smooth_field(wave_key, phase_key, amplitude):
    keys_x, keys_y, keys_z = jax.random.split(wave_key, 3)
    cycles_x = jax.random.randint(keys_x, (3, 3), 1, max(2, NX // 32 + 1))
    cycles_y = jax.random.randint(keys_y, (3, 3), 1, max(2, NY // 32 + 1))
    cycles_z = jax.random.randint(keys_z, (3, 3), 1, max(2, NZ // 32 + 1))
    offsets = jax.random.uniform(phase_key, (3, 3), jnp.float32, -jnp.pi, jnp.pi)
    total = jnp.zeros((3, NX, NY, NZ), jnp.float32)
    for wave in range(3):
        phase_x = phase_along(cycles_x[:, wave], NX)
        phase_y = phase_along(cycles_y[:, wave], NY)
        phase_z = phase_along(cycles_z[:, wave], NZ)
        angle = 2.0 * jnp.pi * (phase_x[:, :, None, None] + phase_y[:, None, :, None] + phase_z[:, None, None, :])
        total = total + amplitude * jnp.sin(angle + offsets[:, wave][:, None, None, None])
    return total


def draw_velocity(key, part):
    key = jax.random.fold_in(key, 11)
    rough_key, wave_key, phase_key = jax.random.split(key, 3)
    rough = 0.6 * jnp.clip(jax.random.normal(rough_key, (3, NX, NY, NZ), jnp.float32), -3.0, 3.0)
    amplitude = 0.9
    return (rough + smooth_field(wave_key, phase_key, amplitude)).astype(jnp.float32)


def draw_positions(key, part):
    key = jax.random.fold_in(key, 13)
    coords = jnp.clip(6.0 * jax.random.normal(key, (3, P_TOTAL), jnp.float32), -16.0, 16.0)
    return coords.astype(jnp.float32)


def touch_ends(entries, key, low, largest):
    longest = entries.shape.index(max(entries.shape))
    spots = []
    for shift in (0, 1):
        where = [jax.random.randint(jax.random.fold_in(key, axis), (), 0, length) for axis, length in enumerate(entries.shape)]
        where[longest] = (where[longest] + shift) % entries.shape[longest]
        spots.append(tuple(where))
    return entries.at[spots[0]].set(low).at[spots[1]].set(largest)


def levels(key, extent, cuts, least, high):
    def one(dim, blocks):
        draws = jax.random.uniform(jax.random.fold_in(jax.random.fold_in(key, 6), dim), (blocks,), jnp.float32, least / len(cuts), high / len(cuts))
        return jnp.repeat(jnp.exp(draws), extent[dim] // blocks).reshape((-1,) + (1,) * (len(extent) - dim - 1))

    factor_of = one(*cuts[0])
    for cut in cuts[1:]:
        factor_of = factor_of * one(*cut)
    return factor_of


def setup_inputs(seed: int = 0) -> dict:
    splits = jax.random.split(jax.random.key(seed), 7)
    return {
        "velocity": draw_velocity(jax.random.fold_in(splits[6], 71), 0),
        "viscosity": jnp.clip(jnp.exp(math.log(2.0) - 2.3025851 * jax.random.uniform(splits[1], (NX, NY, NZ), jnp.float32) ** levels(splits[1], (NX, NY, NZ), ((0, 32), (2, 8)), -0.2, 0.2)), 0.2, 2.0),
        "positions": draw_positions(jax.random.fold_in(splits[6], 71), 0),
        "weights": jnp.clip(0.049804688 * jax.random.uniform(splits[3], (P_TOTAL, 128), jnp.float32) ** levels(splits[3], (P_TOTAL, 128), ((0, 256),), -0.2, 0.2), 0.0, 0.049804688).astype(jnp.bfloat16),
        "tile_index": draw_tile_index(jax.random.fold_in(splits[6], 71), 0),
        "links": touch_ends(jax.random.randint(splits[5], (P_TOTAL, 2), 0, P_GRP), jax.random.fold_in(splits[5], 1), 0, P_GRP - 1).astype(jnp.int32),
    }


def diffuse(padded_vel, padded_mu):
    center = padded_vel[:, 1:-1, 1:-1, 1:-1]
    mu_center = padded_mu[1:-1, 1:-1, 1:-1]
    summed = jnp.zeros_like(center)
    for direction in range(3):
        below = [slice(1, -1)] * 3
        above = [slice(1, -1)] * 3
        below[direction] = slice(0, -2)
        above[direction] = slice(2, None)
        vel_low = padded_vel[(slice(None),) + tuple(below)]
        vel_high = padded_vel[(slice(None),) + tuple(above)]
        face_low = 0.5 * (mu_center + padded_mu[tuple(below)])
        face_high = 0.5 * (mu_center + padded_mu[tuple(above)])
        summed = summed + face_high * (vel_high - center) - face_low * (center - vel_low)
    return summed


def to_tiles(field, size_x, size_y, size_z):
    shaped = field.reshape(3, size_x // 4, 4, size_y // 4, 4, size_z // 8, 8)
    return shaped.transpose(1, 3, 5, 0, 2, 4, 6).reshape(-1, 3, 128)


def from_tiles(rows, size_x, size_y, size_z):
    shaped = rows.reshape(size_x // 4, size_y // 4, size_z // 8, 3, 4, 4, 8)
    return shaped.transpose(3, 0, 4, 1, 5, 2, 6).reshape(3, size_x, size_y, size_z)


def reference(velocity, viscosity, positions, weights, tile_index, links):
    padded_vel = jnp.pad(velocity, ((0, 0), (1, 1), (1, 1), (1, 1)))
    padded_mu = jnp.pad(viscosity, 1)
    pieces = []
    for start in range(0, NX, 16):
        pieces.append(diffuse(padded_vel[:, start:start + 18], padded_mu[start:start + 18]))
    viscous = jnp.concatenate(pieces, axis=1)
    slabs = []
    moved_all = []
    force_all = []
    for group in range(N_GRP):
        slab = velocity[:, :, :, group * CZ:(group + 1) * CZ]
        tile_vel = to_tiles(slab, NX, NY, CZ).astype(jnp.bfloat16)
        lo_row = group * P_GRP
        grp_w = weights[lo_row:lo_row + P_GRP]
        grp_t = tile_index[lo_row:lo_row + P_GRP]
        grp_l = links[lo_row:lo_row + P_GRP]
        grp_x = positions[:, lo_row:lo_row + P_GRP]
        picked = tile_vel[grp_t]
        point_vel = jnp.einsum("pc,pkc->kp", grp_w.astype(jnp.float32), picked.astype(jnp.float32))
        moved = grp_x + 0.5 * point_vel
        force = moved[:, grp_l[:, 0]] + moved[:, grp_l[:, 1]] - 2.0 * moved
        spread_rows = (force.T[:, :, None] * grp_w.astype(jnp.float32)[:, None, :]).astype(jnp.bfloat16)
        tile_force = jax.ops.segment_sum(spread_rows.astype(jnp.float32), grp_t, num_segments=TILES_SLAB)
        slabs.append(from_tiles(tile_force, NX, NY, CZ))
        moved_all.append(moved)
        force_all.append(force)
    force_field = jnp.concatenate(slabs, axis=3)
    new_velocity = velocity + 0.05 * (viscous + force_field)
    return new_velocity, jnp.concatenate(moved_all, axis=1), jnp.concatenate(force_all, axis=1)
```

```python
import jax
import jax.numpy as jnp
from jax import lax
from jax.experimental import pallas as pl
from jax.experimental.pallas import tpu as pltpu
from jax.sharding import PartitionSpec as P

F32, BF, I32 = jnp.float32, jnp.bfloat16, jnp.int32
DEVS, CAP, PTS = 32, 16, 128
SLOTS = DEVS * CAP
CHUNK_B = 64
CHUNK_C = 128


def iota(shape, dim):
    return lax.broadcasted_iota(I32, shape, dim)


def hot(cond):
    return jnp.where(cond, 1.0, 0.0).astype(BF)


def mm(a, b):
    return jnp.dot(a, b, preferred_element_type=F32)


def mm_nt(a, b):
    return lax.dot_general(a, b, (((1,), (1,)), ((), ())), preferred_element_type=F32)


def split2(x):
    hi = x.astype(BF)
    return hi, (x - hi.astype(F32)).astype(BF)


def split3(x):
    hi = x.astype(BF)
    rest = x - hi.astype(F32)
    mid = rest.astype(BF)
    return hi, mid, (rest - mid.astype(F32)).astype(BF)


F_TXTY, F_TZ, F_SELF, F_ALO, F_AHI, F_BLO, F_BHI = range(7)


def dispatch_kernel(tile_ref, links_ref, pos_ref, w_ref, out_ref):
    tile = tile_ref[...]
    owner = tile >> 9
    local = tile & 511
    owned = hot(iota((DEVS, PTS), 0) == owner)
    before = hot(iota((PTS, PTS), 0) < iota((PTS, PTS), 1))
    rank = jnp.sum(owned.astype(F32) * mm(owned, before), axis=0, keepdims=True).astype(I32)
    code = owner * CAP + rank
    place = hot(iota((SLOTS, PTS), 0) == code)
    out_ref[:, 0:16, :] = mm(place, w_ref[...]).astype(BF).reshape(DEVS, CAP, PTS)
    a, b = links_ref[0:1, :], links_ref[1:2, :]
    fields = [local >> 4, local & 15, iota((1, PTS), 1), a & 127, a >> 7, b & 127, b >> 7, jnp.zeros((1, PTS), I32)]
    reps = jnp.concatenate([jnp.broadcast_to(f, (CAP, PTS)) for f in fields], axis=0)
    values = jnp.where((iota((PTS, PTS), 0) & 15) == rank, reps, 0).astype(F32).astype(BF)
    field_rows = mm_nt(owned, values)
    pos = pos_ref[...]
    hi = pos.astype(BF).astype(F32)
    lo = (pos - hi).astype(BF).astype(F32)
    row = iota((8, PTS), 0)
    block = jnp.zeros((8, PTS), F32)
    for c in range(3):
        block = jnp.where(row == c, hi[c:c + 1], block)
        block = jnp.where(row == c + 4, lo[c:c + 1], block)
    block = jnp.where(row == 3, (code - 256).astype(F32), block)
    tail = jnp.where(iota((DEVS, 8, PTS), 1) == 7, field_rows[:, None, :], block[None])
    out_ref[:, 16:24, :] = tail.astype(BF)


def slot_fields(tail, first, rows):
    source = (first + iota((rows, 8 * DEVS), 0)) >> 4
    pick = hot(iota((rows, 8 * DEVS), 1) == source * 8 + 7)
    found = mm(pick, tail)
    mine = (iota((rows, PTS), 1) & 15) == (iota((rows, PTS), 0) & 15)
    return jnp.where(mine, found, 0.0).astype(BF)


def field_spread(names):
    row = iota((PTS, PTS), 0) >> 4
    return jnp.concatenate([hot(row == f) for f in names], axis=1)


def fill_expand(ref):
    k = iota((PTS, PTS), 0)
    z = iota((PTS, PTS), 1) & 7
    for xy in range(16):
        ref[:, xy * PTS:(xy + 1) * PTS] = hot(k == xy * 8 + z)


def velocity_kernel(pay_ref, vel_ref, out_ref, planes_ref, expand_ref):
    for c in range(3):
        for x in range(4):
            for tx in range(2):
                planes_ref[x, tx * 64:tx * 64 + 64, c * PTS:(c + 1) * PTS] = vel_ref[c, 4 * tx + x].astype(BF)
    fill_expand(expand_ref)
    tail = pay_ref[:, 16:24, :].astype(F32).reshape(8 * DEVS, PTS).astype(BF)
    spread = field_spread((F_TXTY, F_TZ))
    comps = hot((iota((3 * PTS, PTS), 0) >> 7) == (iota((3 * PTS, PTS), 1) & 3))
    n = CHUNK_B
    lane = iota((n, PTS), 1)

    def body(step, total):
        first = step * n
        fields = slot_fields(tail, first, n)
        wide = mm(fields, spread)
        low_row = (wide[:, :PTS] * 4.0).astype(I32)
        in_z = (lane >> 3) == wide[:, PTS:].astype(I32)
        w = pay_ref[pl.ds(step * (n // CAP), n // CAP), 0:16, :].reshape(n, PTS)
        hots = jnp.concatenate([hot(lane == low_row + y) for y in range(4)], axis=0)
        acc = jnp.zeros((n, 3 * PTS), F32)
        for x in range(4):
            cells = mm(hots, planes_ref[x])
            for y in range(4):
                xy = x * 4 + y
                w_xy = jnp.where(in_z, mm(w, expand_ref[:, xy * PTS:(xy + 1) * PTS]), 0.0)
                acc = acc + cells[y * n:(y + 1) * n] * jnp.concatenate([w_xy] * 3, axis=1)
        hi, lo = split2(acc)
        found = mm(hi, comps) + mm(lo, comps)
        mine = (lane >> 2) == ((first + iota((n, PTS), 0)) >> 4)
        vals = jnp.where(mine, found, 0.0).astype(BF)
        slot = hot((iota((CAP, n), 1) & 15) == iota((CAP, n), 0))
        return total + mm(slot, vals)

    total = lax.fori_loop(0, SLOTS // n, body, jnp.zeros((CAP, PTS), F32)).astype(BF)
    out_ref[...] = jnp.broadcast_to(total[None], (DEVS, CAP, PTS))


def post_kernel(me_ref, vals_ref, pay_ref, links_ref, pos_ref, base_ref, vel_out, moved_out, force_out,
                valst_ref, codes_ref, dense_ref, expand_ref, field_ref):
    fill_expand(expand_ref)
    tail = pay_ref[:, 16:24, :].astype(F32).reshape(8 * DEVS, PTS).astype(BF)
    r0, r1 = iota((PTS, 8 * DEVS), 0), iota((PTS, 8 * DEVS), 1)
    pick_x = hot(((r0 >> 2) == (r1 >> 3)) & ((r0 & 3) == (r1 & 3)) & ((r0 & 3) < 3))
    x_all = mm(pick_x, tail)
    pick_code = hot(iota((DEVS, 8 * DEVS), 1) == iota((DEVS, 8 * DEVS), 0) * 8 + 3)
    codes_ref[...] = (mm(pick_code, tail) + 256.0).astype(I32)
    valst_ref[...] = vals_ref[...].astype(F32).reshape(SLOTS, PTS).T.astype(BF)

    def dense_body(g, carry):
        sub = iota((16, PTS), 0) >> 2
        picks = [hot(iota((SLOTS, PTS), 0) == codes_ref[pl.ds(4 * g + k, 1), :]) for k in range(4)]
        found = mm(valst_ref[pl.ds(16 * g, 16), :], jnp.concatenate(picks, axis=1))
        out = found[:, 0:PTS]
        for k in range(1, 4):
            out = jnp.where(sub == k, found[:, k * PTS:(k + 1) * PTS], out)
        dense_ref[pl.ds(16 * g, 16), :] = out
        return carry

    lax.fori_loop(0, 8, dense_body, 0)
    vel_all = dense_ref[...]
    moved_all = x_all + 0.5 * vel_all
    me = me_ref[0, 0]
    own_rows = hot((iota((8, PTS), 1) == me * 4 + iota((8, PTS), 0)) & (iota((8, PTS), 0) < 3))
    moved = pos_ref[...] + 0.5 * mm(own_rows, vel_all.astype(BF))[0:3]
    moved_out[...] = moved
    parts = jnp.concatenate(split3(moved_all), axis=0)
    row_src = (iota((3 * PTS, PTS), 0) & 127) >> 2
    comp_rows = hot((iota((8, 3 * PTS), 1) & 3) == iota((8, 3 * PTS), 0))
    ends = jnp.zeros((8, PTS), F32)
    for end in range(2):
        link = links_ref[end:end + 1, :]
        found = mm(parts, hot(iota((PTS, PTS), 0) == (link & 127)))
        ends = ends + mm(comp_rows, jnp.where(row_src == (link >> 7), found, 0.0).astype(BF))
    force_out[...] = ends[0:3] - 2.0 * moved
    parts_t = jnp.concatenate(split3(moved_all.T), axis=1)
    k, l = iota((3 * PTS, 3 * PTS), 0), iota((3 * PTS, 3 * PTS), 1)
    comp_one = jnp.where((k & 3) == (l >> 7), 1.0, 0.0)
    comp_wide = jnp.concatenate([comp_one.astype(BF), comp_one.astype(BF), (-2.0 * comp_one).astype(BF)], axis=0)
    spread = field_spread((F_ALO, F_BLO, F_SELF, F_AHI, F_BHI, F_TZ))
    spread_t = hot((iota((PTS, PTS), 1) >> 4) == F_TXTY)
    n = CHUNK_C
    lane = iota((n, PTS), 1)
    lane_src = (iota((n, 3 * PTS), 1) & 127) >> 2
    field_ref[...] = jnp.zeros_like(field_ref)

    def body(step, carry):
        first = step * n
        fields = slot_fields(tail, first, n)
        wide = mm(fields, spread).astype(I32)
        source = (first + iota((n, PTS), 0)) >> 4
        ends = []
        for low, high in ((0, wide[:, 3 * PTS:4 * PTS]), (1, wide[:, 4 * PTS:5 * PTS]), (2, source)):
            found = mm(hot(lane == wide[:, low * PTS:(low + 1) * PTS]), parts_t)
            ends.append(jnp.where(lane_src == jnp.concatenate([high] * 3, axis=1), found, 0.0).astype(BF))
        force = mm(jnp.concatenate(ends, axis=1), comp_wide)
        in_z = (lane >> 3) == wide[:, 5 * PTS:]
        w = pay_ref[pl.ds(step * (n // CAP), n // CAP), 0:16, :].reshape(n, PTS)
        low_row = (mm_nt(spread_t, fields) * 4.0).astype(I32)
        hots = jnp.concatenate([hot(iota((PTS, n), 0) == low_row + y) for y in range(4)], axis=1)
        for x in range(4):
            rows = []
            for y in range(4):
                xy = x * 4 + y
                w_xy = jnp.where(in_z, mm(w, expand_ref[:, xy * PTS:(xy + 1) * PTS]), 0.0)
                rows.append((force * jnp.concatenate([w_xy] * 3, axis=1)).astype(BF))
            field_ref[x] += mm(hots, jnp.concatenate(rows, axis=0))
        return carry

    lax.fori_loop(0, SLOTS // n, body, 0)
    for c in range(3):
        for x in range(4):
            for tx in range(2):
                vel_out[c, 4 * tx + x] = base_ref[c, 4 * tx + x] + 0.05 * field_ref[
                    x, tx * 64:tx * 64 + 64, c * PTS:(c + 1) * PTS]


def faces_kernel(vel_ref, mu_ref, low_ref, high_ref, z_ref):
    for c in range(3):
        low_ref[c] = vel_ref[c, 0].astype(BF)
        high_ref[c] = vel_ref[c, 7].astype(BF)
    low_ref[3] = mu_ref[0].astype(BF)
    high_ref[3] = mu_ref[7].astype(BF)
    row, lane = iota((16, PTS), 0), iota((16, PTS), 1)
    ends = hot(((row < 8) & (lane == 0)) | ((row >= 8) & (lane == PTS - 1)))
    for c in range(4):
        cells = (vel_ref[c] if c < 3 else mu_ref[...]).reshape(512, PTS).astype(BF)
        z_ref[:, :, c * 512:(c + 1) * 512] = mm_nt(ends, cells).astype(BF).reshape(2, 8, 512)


def stencil_kernel(vel_ref, mu_ref, low_ref, high_ref, zlow_ref, zhigh_ref, out_ref):
    row, lane = iota((64, PTS), 0), iota((64, PTS), 1)
    first_lane, last_lane = lane == 0, lane == PTS - 1
    z_low = [zlow_ref[0:8, c * 512:(c + 1) * 512].astype(F32).T.astype(BF) for c in range(4)]
    z_high = [zhigh_ref[0:8, c * 512:(c + 1) * 512].astype(F32).T.astype(BF) for c in range(4)]
    pick_low = hot((iota((8, PTS), 0) == 0) & (iota((8, PTS), 1) == 0))
    pick_high = hot((iota((8, PTS), 0) == 0) & (iota((8, PTS), 1) == PTS - 1))
    h_low = [mm(z, pick_low) for z in z_low]
    h_high = [mm(z, pick_high) for z in z_high]

    def around(c, x):
        def plane(i):
            if i < 0:
                return low_ref[c].astype(F32)
            if i > 7:
                return high_ref[c].astype(F32)
            return vel_ref[c, i] if c < 3 else mu_ref[i]

        u = plane(x)
        y_low = jnp.where(row == 0, 0.0, pltpu.roll(u, 1, 0))
        y_high = jnp.where(row == 63, 0.0, pltpu.roll(u, 63, 0))
        zl = jnp.where(first_lane, 0.0, pltpu.roll(u, 1, 1)) + h_low[c][x * 64:x * 64 + 64]
        zh = jnp.where(last_lane, 0.0, pltpu.roll(u, PTS - 1, 1)) + h_high[c][x * 64:x * 64 + 64]
        return u, (plane(x - 1), plane(x + 1), y_low, y_high, zl, zh)

    for x in range(8):
        mu, mus = around(3, x)
        faces = [0.5 * (mu + m) for m in mus]
        for c in range(3):
            u, us = around(c, x)
            total = jnp.zeros_like(u)
            for face, other in zip(faces, us):
                total = total + face * (other - u)
            out_ref[c, x] = u + 0.05 * total


VMEM = pl.BlockSpec(memory_space=pltpu.VMEM)
SMEM = pl.BlockSpec(memory_space=pltpu.SMEM)


def call(kernel, outs, scratch, cost, *args, specs=None):
    return pl.pallas_call(
        kernel,
        out_shape=[jax.ShapeDtypeStruct(s, d) for s, d in outs],
        in_specs=specs or [VMEM] * len(args),
        out_specs=[VMEM] * len(outs),
        scratch_shapes=scratch,
        compiler_params=pltpu.CompilerParams(vmem_limit_bytes=40 * 1024 * 1024),
        cost_estimate=pl.CostEstimate(flops=cost * 1000000, bytes_accessed=cost * 4000, transcendentals=0),
    )(*args)


def shift(x, axis, up):
    count = lax.axis_size(axis)
    pairs = [(i, i + 1) if up else (i + 1, i) for i in range(count - 1)]
    return lax.ppermute(x, axis, pairs)


def on_device(velocity, viscosity, positions, weights, tile_index, links):
    me = lax.axis_index("dev").astype(I32).reshape(1, 1)
    links_t = links.T
    (payload,) = call(
        dispatch_kernel, [((DEVS, 24, PTS), BF)], [], 100,
        tile_index.reshape(1, PTS), links_t, positions, weights,
    )
    arrived = lax.all_to_all(payload, "dev", 0, 0, tiled=True)
    face_low, face_high, z_faces = call(
        faces_kernel, [((4, 64, PTS), BF), ((4, 64, PTS), BF), ((2, 8, 2048), BF)], [], 100, velocity, viscosity
    )
    from_low = shift(face_high, "dev", True)
    from_high = shift(face_low, "dev", False)
    z_low = shift(z_faces[1], "grp", True)
    z_high = shift(z_faces[0], "grp", False)
    (values,) = call(
        velocity_kernel, [((DEVS, CAP, PTS), BF)],
        [pltpu.VMEM((4, PTS, 3 * PTS), BF), pltpu.VMEM((PTS, 16 * PTS), BF)], 1000, arrived, velocity,
    )
    all_values = lax.all_to_all(values, "dev", 0, 0, tiled=True)
    (base,) = call(
        stencil_kernel, [((3, 8, 64, PTS), F32)], [], 500, velocity, viscosity, from_low, from_high, z_low, z_high
    )
    return call(
        post_kernel, [((3, 8, 64, PTS), F32), ((3, PTS), F32), ((3, PTS), F32)],
        [pltpu.VMEM((PTS, SLOTS), BF), pltpu.VMEM((DEVS, PTS), I32), pltpu.VMEM((PTS, PTS), F32),
         pltpu.VMEM((PTS, 16 * PTS), BF), pltpu.VMEM((4, PTS, 3 * PTS), F32)], 2000,
        me, all_values, arrived, links_t, positions, base, specs=[SMEM] + [VMEM] * 5,
    )


def solution(mesh):
    in_specs = (
        P(None, "dev", None, "grp"),
        P("dev", None, "grp"),
        P(None, ("grp", "dev")),
        P(("grp", "dev"), None),
        P(("grp", "dev")),
        P(("grp", "dev"), None),
    )
    out_specs = (P(None, "dev", None, "grp"), P(None, ("grp", "dev")), P(None, ("grp", "dev")))
    return jax.shard_map(
        lambda *args: tuple(on_device(*args)), mesh=mesh, in_specs=in_specs, out_specs=out_specs, check_vma=False
    )
```

```python
import jax
import jax.numpy as jnp
from jax import lax
from jax.experimental import pallas as pl
from jax.experimental.pallas import tpu as pltpu
from jax.sharding import PartitionSpec as P

F32, BF, I32 = jnp.float32, jnp.bfloat16, jnp.int32
DEVS, CAP, PTS = 32, 16, 128
SLOTS = DEVS * CAP
TILES = 512


def iota(shape, dim):
    return lax.broadcasted_iota(I32, shape, dim)


def hot(cond):
    return jnp.where(cond, 1.0, 0.0).astype(BF)


def mm(a, b):
    return jnp.dot(a, b, preferred_element_type=F32)


def mm_nt(a, b):
    return lax.dot_general(a, b, (((1,), (1,)), ((), ())), preferred_element_type=F32)


def split2(x):
    hi = x.astype(BF)
    return hi, (x - hi.astype(F32)).astype(BF)


F_TILE, F_SELF, F_ALO, F_AHI, F_BLO, F_BHI = range(6)


def dispatch_kernel(tile_ref, links_ref, pos_ref, w_ref, out_ref):
    tile = tile_ref[...]
    owner = tile >> 9
    local = tile & 511
    owned = hot(iota((DEVS, PTS), 0) == owner)
    before = hot(iota((PTS, PTS), 0) < iota((PTS, PTS), 1))
    rank = jnp.sum(owned.astype(F32) * mm(owned, before), axis=0, keepdims=True).astype(I32)
    code = owner * CAP + rank
    place = hot(iota((SLOTS, PTS), 0) == code)
    out_ref[:, 0:16, :] = mm(place, w_ref[...]).astype(BF).reshape(DEVS, CAP, PTS)
    a, b = links_ref[0:1, :], links_ref[1:2, :]
    order = (local & 15) * 32 + (local >> 4) - 256
    fields = [order, iota((1, PTS), 1), a & 127, a >> 7, b & 127, b >> 7] + [jnp.zeros((1, PTS), I32)] * 2
    reps = jnp.concatenate([jnp.broadcast_to(f, (CAP, PTS)) for f in fields], axis=0)
    values = jnp.where((iota((PTS, PTS), 0) & 15) == rank, reps, 0).astype(F32).astype(BF)
    field_rows = mm_nt(owned, values)
    pos = pos_ref[...]
    hi = pos.astype(BF).astype(F32)
    lo = (pos - hi).astype(BF).astype(F32)
    row = iota((8, PTS), 0)
    block = jnp.zeros((8, PTS), F32)
    for c in range(3):
        block = jnp.where(row == c, hi[c:c + 1], block)
        block = jnp.where(row == c + 4, lo[c:c + 1], block)
    block = jnp.where(row == 3, (code - 256).astype(F32), block)
    tail = jnp.where(iota((DEVS, 8, PTS), 1) == 7, field_rows[:, None, :], block[None])
    out_ref[:, 16:24, :] = tail.astype(BF)


def slot_fields(pay_ref):
    tail = pay_ref[:, 16:24, :].astype(F32).reshape(8 * DEVS, PTS).astype(BF)
    source = iota((SLOTS, 8 * DEVS), 0) >> 4
    found = mm(hot(iota((SLOTS, 8 * DEVS), 1) == source * 8 + 7), tail)
    mine = (iota((SLOTS, PTS), 1) & 15) == (iota((SLOTS, PTS), 0) & 15)
    return jnp.where(mine, found, 0.0).astype(BF), tail


def exchange(parts):
    group = iota(parts[0].shape, 1) >> 3
    for step in (1, 2, 4, 8):
        odd = (group & step) != 0
        out = list(parts)
        for i in range(16):
            if not i & step:
                j = i | step
                out[i] = jnp.where(odd, pltpu.roll(parts[j], 8 * step, 1), parts[i])
                out[j] = jnp.where(odd, parts[j], pltpu.roll(parts[i], PTS - 8 * step, 1))
        parts = out
    return parts


def tiles_kernel(vel_ref, out_ref):
    for c in range(3):
        for tx in range(2):
            rows = [vel_ref[c, 4 * tx + xy // 4, pl.ds(xy % 4, 16, stride=4), :] for xy in range(16)]
            for tz, part in enumerate(exchange(rows)):
                out_ref[tz * 32 + tx * 16:tz * 32 + tx * 16 + 16, c * PTS:(c + 1) * PTS] = part.astype(BF)


def velocity_kernel(pay_ref, tiles_ref, out_ref):
    fields, _ = slot_fields(pay_ref)
    tile = (mm(fields, hot((iota((PTS, PTS), 0) >> 4) == F_TILE)) + 256.0).astype(I32)
    lane = iota((SLOTS, PTS), 1)
    picks = jnp.concatenate([hot(tile == lane + k * PTS) for k in range(TILES // PTS)], axis=1)
    cells = mm(picks, tiles_ref[...])
    w = pay_ref[:, 0:16, :].reshape(SLOTS, PTS).astype(F32)
    hi, lo = split2(cells * jnp.concatenate([w] * 3, axis=1))
    comps = hot((iota((3 * PTS, PTS), 0) >> 7) == (iota((3 * PTS, PTS), 1) & 3))
    found = mm(hi, comps) + mm(lo, comps)
    mine = (lane >> 2) == (iota((SLOTS, PTS), 0) >> 4)
    vals = jnp.where(mine, found, 0.0).astype(BF)
    slot = hot((iota((CAP, SLOTS), 1) & 15) == iota((CAP, SLOTS), 0))
    out_ref[...] = jnp.broadcast_to(mm(slot, vals).astype(BF)[None], (DEVS, CAP, PTS))


def prepare_kernel(pay_ref, spread_ref, comps_ref):
    fields, _ = slot_fields(pay_ref)
    k, l = iota((2 * PTS, 3 * PTS), 0), iota((2 * PTS, 3 * PTS), 1)
    comp = jnp.where((k & 3) == (l >> 7), 1.0, 0.0)
    for e in range(3):
        comps_ref[e * 2 * PTS:(e + 1) * 2 * PTS, :] = ((-2.0 if e == 2 else 1.0) * comp).astype(BF)
    tile = (mm_nt(hot((iota((PTS, PTS), 1) >> 4) == F_TILE), fields) + 256.0).astype(I32)
    for k in range(TILES // PTS):
        spread_ref[k * PTS:(k + 1) * PTS, :] = hot(iota((PTS, SLOTS), 0) + k * PTS == tile)


def post_kernel(me_ref, vals_ref, pay_ref, pos_ref, links_ref, base_ref, vel_ref, mu_ref, low_ref, high_ref,
                zlow_ref, zhigh_ref, spread_ref, comps_ref, vel_out, moved_out, force_out, rows_ref, field_ref):
    fields, tail = slot_fields(pay_ref)
    r0, r1 = iota((PTS, 8 * DEVS), 0), iota((PTS, 8 * DEVS), 1)
    same = (r0 >> 2) == (r1 >> 3)
    x_all = mm(hot(same & ((r0 & 3) == (r1 & 3)) & ((r0 & 3) < 3)), tail)
    code = (mm(hot(same & ((r1 & 7) == 3)), tail) + 256.0).astype(I32)
    vals = vals_ref[...].astype(F32).reshape(SLOTS, PTS).T
    vel_all = jnp.zeros((PTS, PTS), F32)
    for k in range(SLOTS // PTS):
        found = jnp.take_along_axis(vals[:, k * PTS:(k + 1) * PTS], code & 127, axis=1)
        vel_all = jnp.where((code >> 7) == k, found, vel_all)
    moved_all = x_all + 0.5 * vel_all
    parts_t = jnp.concatenate(split2(moved_all.T), axis=1)
    n = PTS
    lane = iota((n, PTS), 1)
    frow = iota((PTS, PTS), 0) >> 4
    names = (F_ALO, F_BLO, F_SELF, F_AHI, F_BHI)
    wide_of = jnp.concatenate([hot(frow == f) for f in names], axis=1)
    for step in range(SLOTS // n):
        rows = slice(step * n, (step + 1) * n)
        wide = mm(fields[rows], wide_of).astype(I32)
        highs = (wide[:, 3 * PTS:4 * PTS], wide[:, 4 * PTS:], (step * n + iota((n, PTS), 0)) >> 4)
        ends = []
        for e in range(3):
            found = mm(hot(lane == wide[:, e * PTS:(e + 1) * PTS]), parts_t).astype(BF)
            ends.append(found * jnp.concatenate([hot((lane >> 2) == highs[e])] * 2, axis=1))
        force = mm(jnp.concatenate(ends, axis=1), comps_ref[...])
        w = pay_ref[step * (n // CAP):(step + 1) * (n // CAP), 0:16, :].reshape(n, PTS).astype(F32)
        rows_ref[rows, :] = (force * jnp.concatenate([w] * 3, axis=1)).astype(BF)
    field_ref[...] = mm(spread_ref[...], rows_ref[...])
    me = me_ref[0, 0]
    own_rows = hot((iota((16, PTS), 1) == me * 4 + iota((16, PTS), 0)) & (iota((16, PTS), 0) < 3))
    moved = pos_ref[...] + 0.5 * mm(own_rows, vel_all.astype(BF))[0:3]
    moved_out[...] = moved
    parts = jnp.concatenate(split2(moved_all), axis=0)
    comp_rows = hot((iota((16, 2 * PTS), 1) & 3) == iota((16, 2 * PTS), 0))
    ends = jnp.zeros((16, PTS), F32)
    for e in range(2):
        link = links_ref[e:e + 1, :]
        found = mm(parts, hot(iota((PTS, PTS), 0) == (link & 127))).astype(BF)
        mask = hot((iota((PTS, PTS), 0) >> 2) == (link >> 7))
        ends = ends + mm(comp_rows, found * jnp.concatenate([mask] * 2, axis=0))
    force_out[...] = ends[0:3] - 2.0 * moved
    for c in range(3):
        for tx in range(2):
            rows = [field_ref[tz * 32 + tx * 16:tz * 32 + tx * 16 + 16, c * PTS:(c + 1) * PTS] for tz in range(16)]
            for xy, part in enumerate(exchange(rows)):
                where = (c, 4 * tx + xy // 4, pl.ds(xy % 4, 16, stride=4), slice(None))
                vel_out[where] = base_ref[where] + 0.05 * part
    row, lane = iota((16, PTS), 0), iota((16, PTS), 1)
    ends = hot(((row == 0) & (lane == 0)) | ((row == 8) & (lane == PTS - 1)))
    beyond = []
    for c in range(4):
        z = jnp.concatenate([ref[:, c * 512:(c + 1) * 512].astype(F32) for ref in (zlow_ref, zhigh_ref)], axis=0)
        beyond.append(mm(z.T.astype(BF), ends))
    lane = iota((64, PTS), 1)
    outer = jnp.where((lane == 0) | (lane == PTS - 1), 0.025, 0.0)
    for x in range(8):
        mu = mu_ref[x]
        part = slice(x * 64, x * 64 + 64)
        face = outer * (mu + beyond[3][part])
        halo = {0: low_ref, 7: high_ref}.get(x)
        face_x = None if halo is None else 0.025 * (mu + halo[3].astype(F32))
        for c in range(3):
            u = vel_ref[c, x]
            more = face * (beyond[c][part] - u)
            if halo is not None:
                more = more + face_x * (halo[c].astype(F32) - u)
            vel_out[c, x] = vel_out[c, x] + more


def faces_kernel(vel_ref, mu_ref, low_ref, high_ref, z_ref):
    for c in range(3):
        low_ref[c] = vel_ref[c, 0].astype(BF)
        high_ref[c] = vel_ref[c, 7].astype(BF)
    low_ref[3] = mu_ref[0].astype(BF)
    high_ref[3] = mu_ref[7].astype(BF)
    row, lane = iota((16, PTS), 0), iota((16, PTS), 1)
    ends = hot(((row < 8) & (lane == 0)) | ((row >= 8) & (lane == PTS - 1)))
    for c in range(4):
        cells = (vel_ref[c] if c < 3 else mu_ref[...]).reshape(512, PTS).astype(BF)
        z_ref[:, :, c * 512:(c + 1) * 512] = mm_nt(ends, cells).astype(BF).reshape(2, 8, 512)


def stencil_kernel(vel_ref, mu_ref, out_ref):
    row, lane = iota((64, PTS), 0), iota((64, PTS), 1)

    def plane(c, i):
        return vel_ref[c, i] if c < 3 else mu_ref[i]

    def around(c, x):
        u = plane(c, x)
        out = [
            pltpu.roll(u, 1, 1),
            pltpu.roll(u, PTS - 1, 1),
            jnp.where(row == 0, 0.0, pltpu.roll(u, 1, 0)),
            jnp.where(row == 63, 0.0, pltpu.roll(u, 63, 0)),
        ]
        return u, out + [plane(c, i) for i in (x - 1, x + 1) if 0 <= i < 8]

    inner = [jnp.where(lane == 0, 0.0, 0.025), jnp.where(lane == PTS - 1, 0.0, 0.025)] + [0.025] * 4
    for x in range(8):
        mu, mus = around(3, x)
        faces = [scale * (mu + m) for scale, m in zip(inner, mus)]
        for c in range(3):
            u, us = around(c, x)
            total = u
            for face, other in zip(faces, us):
                total = total + face * (other - u)
            out_ref[c, x] = total


VMEM = pl.BlockSpec(memory_space=pltpu.VMEM)
SMEM = pl.BlockSpec(memory_space=pltpu.SMEM)


def call(kernel, outs, scratch, cost, *args, specs=None):
    return pl.pallas_call(
        kernel,
        out_shape=[jax.ShapeDtypeStruct(s, d) for s, d in outs],
        in_specs=specs or [VMEM] * len(args),
        out_specs=[VMEM] * len(outs),
        scratch_shapes=scratch,
        compiler_params=pltpu.CompilerParams(vmem_limit_bytes=40 * 1024 * 1024),
        cost_estimate=pl.CostEstimate(flops=cost * 1000000, bytes_accessed=cost * 4000, transcendentals=0),
    )(*args)


def shift(x, axis, up):
    count = lax.axis_size(axis)
    pairs = [(i, i + 1) if up else (i + 1, i) for i in range(count - 1)]
    return lax.ppermute(x, axis, pairs)


def on_device(velocity, viscosity, positions, weights, tile_index, links):
    me = lax.axis_index("dev").astype(I32).reshape(1, 1)
    links_t = links.T
    (payload,) = call(
        dispatch_kernel, [((DEVS, 24, PTS), BF)], [], 100,
        tile_index.reshape(1, PTS), links_t, positions, weights,
    )
    arrived = lax.all_to_all(payload, "dev", 0, 0, tiled=True)
    face_low, face_high, z_faces = call(
        faces_kernel, [((4, 64, PTS), BF), ((4, 64, PTS), BF), ((2, 8, 2048), BF)], [], 100, velocity, viscosity
    )
    from_low = shift(face_high, "dev", True)
    from_high = shift(face_low, "dev", False)
    (tiles,) = call(tiles_kernel, [((TILES, 3 * PTS), BF)], [], 300, velocity)
    (base,) = call(stencil_kernel, [((3, 8, 64, PTS), F32)], [], 500, velocity, viscosity)
    arrived, tiles, base, z_faces = lax.optimization_barrier((arrived, tiles, base, z_faces))
    (values,) = call(velocity_kernel, [((DEVS, CAP, PTS), BF)], [], 500, arrived, tiles)
    all_values = lax.all_to_all(values, "dev", 0, 0, tiled=True)
    z_faces, arrived, values = lax.optimization_barrier((z_faces, arrived, values))
    z_low = shift(z_faces[1], "grp", True)
    z_high = shift(z_faces[0], "grp", False)
    prepared = call(prepare_kernel, [((TILES, SLOTS), BF), ((6 * PTS, 3 * PTS), BF)], [], 500, arrived)
    return call(
        post_kernel, [((3, 8, 64, PTS), F32), ((3, PTS), F32), ((3, PTS), F32)],
        [pltpu.VMEM((SLOTS, 3 * PTS), BF), pltpu.VMEM((TILES, 3 * PTS), F32)], 1000,
        me, all_values, arrived, positions, links_t, base, velocity, viscosity, from_low, from_high, z_low, z_high,
        *prepared, specs=[SMEM] + [VMEM] * 13,
    )


def solution(mesh):
    in_specs = (
        P(None, "dev", None, "grp"),
        P("dev", None, "grp"),
        P(None, ("grp", "dev")),
        P(("grp", "dev"), None),
        P(("grp", "dev")),
        P(("grp", "dev"), None),
    )
    out_specs = (P(None, "dev", None, "grp"), P(None, ("grp", "dev")), P(None, ("grp", "dev")))
    return jax.shard_map(
        lambda *args: tuple(on_device(*args)), mesh=mesh, in_specs=in_specs, out_specs=out_specs, check_vma=False
    )
```

```python
import jax
import jax.numpy as jnp
from jax import lax
from jax.experimental import pallas as pl
from jax.experimental.pallas import tpu as pltpu
from jax.sharding import PartitionSpec as P

F32, BF, I32 = jnp.float32, jnp.bfloat16, jnp.int32
DEVS, CAP, PTS = 32, 16, 128
SLOTS = DEVS * CAP
TILES = 512


def iota(shape, dim):
    return lax.broadcasted_iota(I32, shape, dim)


def hot(cond):
    return jnp.where(cond, 1.0, 0.0).astype(BF)


def mm(a, b):
    return jnp.dot(a, b, preferred_element_type=F32)


def mm_nt(a, b):
    return lax.dot_general(a, b, (((1,), (1,)), ((), ())), preferred_element_type=F32)


def split2(x):
    hi = x.astype(BF)
    return hi, (x - hi.astype(F32)).astype(BF)


F_TILE, F_SELF, F_ALO, F_AHI, F_BLO, F_BHI = range(6)


def dispatch_kernel(tile_hbm, links_hbm, pos_hbm, w_hbm, out_ref, tile_ref, links_ref, pos_ref, w_ref, sems):
    copies = [
        pltpu.make_async_copy(src, dst, sems.at[i])
        for i, (src, dst) in enumerate(
            ((tile_hbm, tile_ref), (links_hbm, links_ref), (w_hbm, w_ref), (pos_hbm, pos_ref))
        )
    ]
    for copy in copies:
        copy.start()
    for copy in copies:
        copy.wait()
    tile = tile_ref[...]
    owner = tile >> 9
    local = tile & 511
    owned = hot(iota((DEVS, PTS), 0) == owner)
    before = hot(iota((PTS, PTS), 0) < iota((PTS, PTS), 1))
    rank = jnp.sum(owned.astype(F32) * mm(owned, before), axis=0, keepdims=True).astype(I32)
    code = owner * CAP + rank
    place = hot(iota((SLOTS, PTS), 0) == code)
    out_ref[:, 0:16, :] = mm(place, w_ref[...]).astype(BF).reshape(DEVS, CAP, PTS)
    a, b = links_ref[0:1, :], links_ref[1:2, :]
    order = (local & 15) * 32 + (local >> 4) - 256
    fields = [order, iota((1, PTS), 1), a & 127, a >> 7, b & 127, b >> 7] + [jnp.zeros((1, PTS), I32)] * 2
    reps = jnp.concatenate([jnp.broadcast_to(f, (CAP, PTS)) for f in fields], axis=0)
    values = jnp.where((iota((PTS, PTS), 0) & 15) == rank, reps, 0).astype(F32).astype(BF)
    field_rows = mm_nt(owned, values)
    pos = pos_ref[...]
    hi = pos.astype(BF).astype(F32)
    lo = (pos - hi).astype(BF).astype(F32)
    row = iota((8, PTS), 0)
    block = jnp.zeros((8, PTS), F32)
    for c in range(3):
        block = jnp.where(row == c, hi[c:c + 1], block)
        block = jnp.where(row == c + 4, lo[c:c + 1], block)
    block = jnp.where(row == 3, (code - 256).astype(F32), block)
    tail = jnp.where(iota((DEVS, 8, PTS), 1) == 7, field_rows[:, None, :], block[None])
    out_ref[:, 16:24, :] = tail.astype(BF)


def slot_fields(pay_ref):
    block = pay_ref[:, 16:24, :].astype(F32)
    found = jnp.broadcast_to(block[:, 7:8, :], (DEVS, CAP, PTS)).reshape(SLOTS, PTS)
    mine = (iota((SLOTS, PTS), 1) & 15) == (iota((SLOTS, PTS), 0) & 15)
    return jnp.where(mine, found, 0.0).astype(BF), block.reshape(8 * DEVS, PTS).astype(BF)


def exchange(parts):
    group = iota(parts[0].shape, 1) >> 3
    for step in (1, 2, 4, 8):
        odd = (group & step) != 0
        out = list(parts)
        for i in range(16):
            if not i & step:
                j = i | step
                out[i] = jnp.where(odd, pltpu.roll(parts[j], 8 * step, 1), parts[i])
                out[j] = jnp.where(odd, parts[j], pltpu.roll(parts[i], PTS - 8 * step, 1))
        parts = out
    return parts


def tiles_kernel(vel_ref, out_ref):
    for c in range(3):
        for tx in range(2):
            rows = [vel_ref[c, 4 * tx + xy // 4, pl.ds(xy % 4, 16, stride=4), :] for xy in range(16)]
            for tz, part in enumerate(exchange(rows)):
                out_ref[tz * 32 + tx * 16:tz * 32 + tx * 16 + 16, c * PTS:(c + 1) * PTS] = part.astype(BF)


def velocity_kernel(pay_ref, tiles_ref, out_ref):
    fields, _ = slot_fields(pay_ref)
    tile = (mm(fields, hot((iota((PTS, PTS), 0) >> 4) == F_TILE)) + 256.0).astype(I32)
    lane = iota((SLOTS, PTS), 1)
    picks = jnp.concatenate([hot(tile == lane + k * PTS) for k in range(TILES // PTS)], axis=1)
    cells = mm(picks, tiles_ref[...])
    w = pay_ref[:, 0:16, :].reshape(SLOTS, PTS).astype(F32)
    hi, lo = split2(cells * jnp.concatenate([w] * 3, axis=1))
    comps = hot((iota((3 * PTS, PTS), 0) >> 7) == (iota((3 * PTS, PTS), 1) & 3))
    found = mm(hi, comps) + mm(lo, comps)
    mine = (lane >> 2) == (iota((SLOTS, PTS), 0) >> 4)
    vals = jnp.where(mine, found, 0.0).astype(BF)
    slot = hot((iota((CAP, SLOTS), 1) & 15) == iota((CAP, SLOTS), 0))
    out_ref[...] = jnp.broadcast_to(mm(slot, vals).astype(BF)[None], (DEVS, CAP, PTS))


def prepare_kernel(pay_ref, spread_ref, comps_ref):
    fields, _ = slot_fields(pay_ref)
    k, l = iota((2 * PTS, 3 * PTS), 0), iota((2 * PTS, 3 * PTS), 1)
    comp = jnp.where((k & 3) == (l >> 7), 1.0, 0.0)
    for e in range(3):
        comps_ref[e * 2 * PTS:(e + 1) * 2 * PTS, :] = ((-2.0 if e == 2 else 1.0) * comp).astype(BF)
    tile = (mm_nt(hot((iota((PTS, PTS), 1) >> 4) == F_TILE), fields) + 256.0).astype(I32)
    for k in range(TILES // PTS):
        spread_ref[k * PTS:(k + 1) * PTS, :] = hot(iota((PTS, SLOTS), 0) + k * PTS == tile)


def post_kernel(me_ref, vals_ref, pay_ref, pos_ref, links_ref, base_ref, vel_ref, mu_ref, xa_ref, xb_ref,
                za_ref, zb_ref, spread_ref, comps_ref, vel_out, moved_out, force_out,
                rows_ref, field_ref, new_ref, sems):
    fields, tail = slot_fields(pay_ref)
    r0, r1 = iota((PTS, 8 * DEVS), 0), iota((PTS, 8 * DEVS), 1)
    same = (r0 >> 2) == (r1 >> 3)
    x_all = mm(hot(same & ((r0 & 3) == (r1 & 3)) & ((r0 & 3) < 3)), tail)
    code = (mm(hot(same & ((r1 & 7) == 3)), tail) + 256.0).astype(I32)
    vals = vals_ref[...].astype(F32).reshape(SLOTS, PTS).T
    vel_all = jnp.zeros((PTS, PTS), F32)
    for k in range(SLOTS // PTS):
        found = jnp.take_along_axis(vals[:, k * PTS:(k + 1) * PTS], code & 127, axis=1)
        vel_all = jnp.where((code >> 7) == k, found, vel_all)
    moved_all = x_all + 0.5 * vel_all
    parts_t = jnp.concatenate(split2(moved_all.T), axis=1)
    frow = iota((PTS, PTS), 0) >> 4
    names = (F_ALO, F_BLO, F_SELF, F_AHI, F_BHI)
    wide = mm(fields, jnp.concatenate([hot(frow == f) for f in names], axis=1))
    lane = iota((SLOTS, PTS), 1).astype(F32)
    lane_src = (iota((SLOTS, PTS), 1) >> 2).astype(F32)
    highs = (wide[:, 3 * PTS:4 * PTS], wide[:, 4 * PTS:], (iota((SLOTS, PTS), 0) >> 4).astype(F32))
    ends = []
    for e in range(3):
        found = mm(hot(lane == wide[:, e * PTS:(e + 1) * PTS]), parts_t).astype(BF)
        ends.append(found * jnp.concatenate([hot(lane_src == highs[e])] * 2, axis=1))
    force = mm(jnp.concatenate(ends, axis=1), comps_ref[...])
    w = pay_ref[:, 0:16, :].reshape(SLOTS, PTS).astype(F32)
    rows_ref[...] = (force * jnp.concatenate([w] * 3, axis=1)).astype(BF)
    field_ref[...] = mm(spread_ref[...], rows_ref[...])
    me = me_ref[0, 0]
    own_rows = hot((iota((16, PTS), 1) == me * 4 + iota((16, PTS), 0)) & (iota((16, PTS), 0) < 3))
    moved = pos_ref[...] + 0.5 * mm(own_rows, vel_all.astype(BF))[0:3]
    moved_out[...] = moved
    parts = jnp.concatenate(split2(moved_all), axis=0)
    comp_rows = hot((iota((16, 2 * PTS), 1) & 3) == iota((16, 2 * PTS), 0))
    ends = jnp.zeros((16, PTS), F32)
    for e in range(2):
        link = links_ref[e:e + 1, :]
        found = mm(parts, hot(iota((PTS, PTS), 0) == (link & 127))).astype(BF)
        mask = hot((iota((PTS, PTS), 0) >> 2) == (link >> 7))
        ends = ends + mm(comp_rows, found * jnp.concatenate([mask] * 2, axis=0))
    force_out[...] = ends[0:3] - 2.0 * moved
    row, lane = iota((16, PTS), 0), iota((16, PTS), 1)
    first, second = pair_ends(me_ref[0, 1])
    ends = hot(((row == 0) & (lane == first * (PTS - 1))) | ((row == 8) & (lane == second * (PTS - 1))))
    wide_row = iota((16, 512), 0)
    beyond = []
    for c in range(4):
        za, zb = [
            jnp.concatenate([ref[c * 4 + k:c * 4 + k + 1, :].astype(F32) for k in range(4)], axis=1)
            for ref in (za_ref, zb_ref)
        ]
        z = jnp.where(wide_row == 0, za, jnp.where(wide_row == 8, zb, 0.0))
        beyond.append(mm(z.T.astype(BF), ends))
    lane = iota((64, PTS), 1)
    outer = jnp.where((lane == 0) | (lane == PTS - 1), 0.025, 0.0)
    face_z = [outer * (mu_ref[x] + beyond[3][x * 64:x * 64 + 64]) for x in range(8)]
    sides = [(end * 7, ref) for end, ref in zip(pair_ends(me_ref[0, 0]), (xa_ref, xb_ref))]
    face_x = [0.025 * (mu_ref[x] + ref[3].astype(F32)) for x, ref in sides]
    copies = []
    for c in range(3):
        for tx in range(2):
            rows = [field_ref[tz * 32 + tx * 16:tz * 32 + tx * 16 + 16, c * PTS:(c + 1) * PTS] for tz in range(16)]
            for xy, part in enumerate(exchange(rows)):
                new_ref[c, 4 * tx + xy // 4, pl.ds(xy % 4, 16, stride=4), :] = part
        for x in range(8):
            beyond_z = beyond[c][x * 64:x * 64 + 64] - vel_ref[c, x]
            new_ref[c, x] = base_ref[c, x] + 0.05 * new_ref[c, x] + face_z[x] * beyond_z
        for (x, ref), face in zip(sides, face_x):
            new_ref[c, x] = new_ref[c, x] + face * (ref[c].astype(F32) - vel_ref[c, x])
        copies.append(pltpu.make_async_copy(new_ref.at[c], vel_out.at[c], sems.at[c]))
        copies[-1].start()
    for copy in copies:
        copy.wait()


def pair_ends(index):
    first = 1 - (index & 1)
    return first, 1 - first


def faces_kernel(me_ref, vel_ref, mu_ref, xa_ref, xb_ref, za_ref, zb_ref):
    for end, ref in zip(pair_ends(me_ref[0, 0]), (xa_ref, xb_ref)):
        for c in range(3):
            ref[c] = vel_ref[c, end * 7].astype(BF)
        ref[3] = mu_ref[end * 7].astype(BF)
    row, lane = iota((16, PTS), 0), iota((16, PTS), 1)
    first, second = pair_ends(me_ref[0, 1])
    ends = hot(((row < 8) & (lane == first * (PTS - 1))) | ((row >= 8) & (lane == second * (PTS - 1))))
    for c in range(4):
        cells = (vel_ref[c] if c < 3 else mu_ref[...]).reshape(512, PTS).astype(BF)
        found = mm_nt(ends, cells).astype(BF)
        for k in range(4):
            part = slice(k * PTS, (k + 1) * PTS)
            za_ref[c * 4 + k:c * 4 + k + 1, :] = found[0:1, part]
            zb_ref[c * 4 + k:c * 4 + k + 1, :] = found[8:9, part]


def stencil_kernel(vel_ref, mu_ref, out_ref):
    row, lane = iota((64, PTS), 0), iota((64, PTS), 1)

    def plane(c, i):
        return vel_ref[c, i] if c < 3 else mu_ref[i]

    def around(c, x):
        u = plane(c, x)
        out = [
            pltpu.roll(u, 1, 1),
            pltpu.roll(u, PTS - 1, 1),
            jnp.where(row == 0, 0.0, pltpu.roll(u, 1, 0)),
            jnp.where(row == 63, 0.0, pltpu.roll(u, 63, 0)),
        ]
        return u, out + [plane(c, i) for i in (x - 1, x + 1) if 0 <= i < 8]

    inner = [jnp.where(lane == 0, 0.0, 0.025), jnp.where(lane == PTS - 1, 0.0, 0.025)] + [0.025] * 4
    for x in range(8):
        mu, mus = around(3, x)
        faces = [scale * (mu + m) for scale, m in zip(inner, mus)]
        for c in range(3):
            u, us = around(c, x)
            total = u
            for face, other in zip(faces, us):
                total = total + face * (other - u)
            out_ref[c, x] = total


VMEM = pl.BlockSpec(memory_space=pltpu.VMEM)
SMEM = pl.BlockSpec(memory_space=pltpu.SMEM)
HBM = pl.BlockSpec(memory_space=pltpu.HBM)


def call(kernel, outs, scratch, cost, *args, specs=None, out_specs=None):
    return pl.pallas_call(
        kernel,
        out_shape=[jax.ShapeDtypeStruct(s, d) for s, d in outs],
        in_specs=specs or [VMEM] * len(args),
        out_specs=out_specs or [VMEM] * len(outs),
        scratch_shapes=scratch,
        compiler_params=pltpu.CompilerParams(vmem_limit_bytes=16 * 1024 * 1024),
        cost_estimate=pl.CostEstimate(flops=cost * 1000000, bytes_accessed=cost * 4000, transcendentals=0),
    )(*args)


def swap(x, axis, first):
    pairs = []
    for i in range(1 - first, lax.axis_size(axis) - 1, 2):
        pairs += [(i, i + 1), (i + 1, i)]
    return lax.ppermute(x, axis, pairs)


def on_device(velocity, viscosity, positions, weights, tile_index, links):
    me = jnp.stack([lax.axis_index("dev"), lax.axis_index("grp")]).astype(I32).reshape(1, 2)
    links_t = links.T
    (payload,) = call(
        dispatch_kernel, [((DEVS, 24, PTS), BF)],
        [pltpu.VMEM((1, PTS), I32), pltpu.VMEM((2, PTS), I32), pltpu.VMEM((3, PTS), F32), pltpu.VMEM((PTS, PTS), BF),
         pltpu.SemaphoreType.DMA((4,))], 100,
        tile_index.reshape(1, PTS), links_t, positions, weights, specs=[HBM] * 4,
    )
    arrived = lax.all_to_all(payload, "dev", 0, 0, tiled=True)
    xa, xb, za, zb = call(
        faces_kernel, [((4, 64, PTS), BF), ((4, 64, PTS), BF), ((16, PTS), BF), ((16, PTS), BF)], [], 100,
        me, velocity, viscosity, specs=[SMEM, VMEM, VMEM],
    )
    xa = swap(xa, "dev", 1)
    za = swap(za, "grp", 1)
    (tiles,) = call(tiles_kernel, [((TILES, 3 * PTS), BF)], [], 300, velocity)
    (base,) = call(stencil_kernel, [((3, 8, 64, PTS), F32)], [], 500, velocity, viscosity)
    arrived, tiles, base, xa, za, xb, zb = lax.optimization_barrier((arrived, tiles, base, xa, za, xb, zb))
    (values,) = call(velocity_kernel, [((DEVS, CAP, PTS), BF)], [], 500, arrived, tiles)
    all_values = lax.all_to_all(values, "dev", 0, 0, tiled=True)
    xb, zb, arrived, values = lax.optimization_barrier((xb, zb, arrived, values))
    xb = swap(xb, "dev", 0)
    zb = swap(zb, "grp", 0)
    prepared = call(prepare_kernel, [((TILES, SLOTS), BF), ((6 * PTS, 3 * PTS), BF)], [], 500, arrived)
    return call(
        post_kernel, [((3, 8, 64, PTS), F32), ((3, PTS), F32), ((3, PTS), F32)],
        [pltpu.VMEM((SLOTS, 3 * PTS), BF), pltpu.VMEM((TILES, 3 * PTS), F32),
         pltpu.VMEM((3, 8, 64, PTS), F32), pltpu.SemaphoreType.DMA((3,))], 1000,
        me, all_values, arrived, positions, links_t, base, velocity, viscosity, xa, xb, za, zb,
        *prepared, specs=[SMEM] + [VMEM] * 13, out_specs=[HBM, VMEM, VMEM],
    )


def solution(mesh):
    in_specs = (
        P(None, "dev", None, "grp"),
        P("dev", None, "grp"),
        P(None, ("grp", "dev")),
        P(("grp", "dev"), None),
        P(("grp", "dev")),
        P(("grp", "dev"), None),
    )
    out_specs = (P(None, "dev", None, "grp"), P(None, ("grp", "dev")), P(None, ("grp", "dev")))
    return jax.shard_map(
        lambda *args: tuple(on_device(*args)), mesh=mesh, in_specs=in_specs, out_specs=out_specs, check_vma=False
    )
```

```python
import jax
import jax.numpy as jnp
from jax import lax
from jax.experimental import pallas as pl
from jax.experimental.pallas import tpu as pltpu
from jax.sharding import PartitionSpec as P

F32, BF, I32 = jnp.float32, jnp.bfloat16, jnp.int32
DEVS, CAP, PTS = 32, 16, 128
SLOTS = DEVS * CAP
TILES = 512


def iota(shape, dim):
    return lax.broadcasted_iota(I32, shape, dim)


def hot(cond):
    return jnp.where(cond, 1.0, 0.0).astype(BF)


def mm(a, b):
    return jnp.dot(a, b, preferred_element_type=F32)


def mm_nt(a, b):
    return lax.dot_general(a, b, (((1,), (1,)), ((), ())), preferred_element_type=F32)


def split3(x):
    hi = x.astype(BF)
    rest = x - hi.astype(F32)
    mid = rest.astype(BF)
    return hi, mid, (rest - mid.astype(F32)).astype(BF)


def split2(x):
    hi = x.astype(BF)
    return hi, (x - hi.astype(F32)).astype(BF)


F_TILE, F_SELF, F_ALO, F_AHI, F_BLO, F_BHI = range(6)


def dispatch_kernel(tile_hbm, links_hbm, pos_hbm, w_hbm, out_ref, tile_ref, links_ref, pos_ref, w_ref, sems):
    copies = [
        pltpu.make_async_copy(src, dst, sems.at[i])
        for i, (src, dst) in enumerate(
            ((tile_hbm, tile_ref), (links_hbm, links_ref), (w_hbm, w_ref), (pos_hbm, pos_ref))
        )
    ]
    for copy in copies:
        copy.start()
    for copy in copies:
        copy.wait()
    tile = tile_ref[...]
    owner = tile >> 9
    local = tile & 511
    owned = hot(iota((DEVS, PTS), 0) == owner)
    before = hot(iota((PTS, PTS), 0) < iota((PTS, PTS), 1))
    rank = jnp.sum(owned.astype(F32) * mm(owned, before), axis=0, keepdims=True).astype(I32)
    code = owner * CAP + rank
    place = hot(iota((SLOTS, PTS), 0) == code)
    out_ref[:, 0:16, :] = mm(place, w_ref[...]).astype(BF).reshape(DEVS, CAP, PTS)
    a, b = links_ref[0:1, :], links_ref[1:2, :]
    order = (local & 15) * 32 + (local >> 4) - 256
    fields = [order, iota((1, PTS), 1), a & 127, a >> 7, b & 127, b >> 7] + [jnp.zeros((1, PTS), I32)] * 2
    reps = jnp.concatenate([jnp.broadcast_to(f, (CAP, PTS)) for f in fields], axis=0)
    values = jnp.where((iota((PTS, PTS), 0) & 15) == rank, reps, 0).astype(F32).astype(BF)
    field_rows = mm_nt(owned, values)
    pos = pos_ref[...]
    hi = pos.astype(BF).astype(F32)
    lo = (pos - hi).astype(BF).astype(F32)
    row = iota((8, PTS), 0)
    block = jnp.zeros((8, PTS), F32)
    for c in range(3):
        block = jnp.where(row == c, hi[c:c + 1], block)
        block = jnp.where(row == c + 4, lo[c:c + 1], block)
    block = jnp.where(row == 3, (code - 256).astype(F32), block)
    tail = jnp.where(iota((DEVS, 8, PTS), 1) == 7, field_rows[:, None, :], block[None])
    out_ref[:, 16:24, :] = tail.astype(BF)


def slot_fields(pay_ref):
    block = pay_ref[:, 16:24, :].astype(F32)
    found = jnp.broadcast_to(block[:, 7:8, :], (DEVS, CAP, PTS)).reshape(SLOTS, PTS)
    mine = (iota((SLOTS, PTS), 1) & 15) == (iota((SLOTS, PTS), 0) & 15)
    return jnp.where(mine, found, 0.0).astype(BF), block.reshape(8 * DEVS, PTS).astype(BF)


def exchange(parts):
    group = iota(parts[0].shape, 1) >> 3
    for step in (1, 2, 4, 8):
        odd = (group & step) != 0
        out = list(parts)
        for i in range(16):
            if not i & step:
                j = i | step
                out[i] = jnp.where(odd, pltpu.roll(parts[j], 8 * step, 1), parts[i])
                out[j] = jnp.where(odd, parts[j], pltpu.roll(parts[i], PTS - 8 * step, 1))
        parts = out
    return parts


def tiles_kernel(vel_ref, out_ref):
    for c in range(3):
        for tx in range(2):
            rows = [vel_ref[c, 4 * tx + xy // 4, pl.ds(xy % 4, 16, stride=4), :] for xy in range(16)]
            for tz, part in enumerate(exchange(rows)):
                out_ref[tz * 32 + tx * 16:tz * 32 + tx * 16 + 16, c * PTS:(c + 1) * PTS] = part.astype(BF)


def velocity_kernel(pay_ref, tiles_ref, out_ref):
    fields, _ = slot_fields(pay_ref)
    tile = (mm(fields, hot((iota((PTS, PTS), 0) >> 4) == F_TILE)) + 256.0).astype(I32)
    lane = iota((SLOTS, PTS), 1)
    picks = jnp.concatenate([hot(tile == lane + k * PTS) for k in range(TILES // PTS)], axis=1)
    cells = mm(picks, tiles_ref[...])
    w = pay_ref[:, 0:16, :].reshape(SLOTS, PTS).astype(F32)
    hi, lo = split2(cells * jnp.concatenate([w] * 3, axis=1))
    comps = hot((iota((3 * PTS, PTS), 0) >> 7) == (iota((3 * PTS, PTS), 1) & 3))
    found = mm(hi, comps) + mm(lo, comps)
    mine = (lane >> 2) == (iota((SLOTS, PTS), 0) >> 4)
    vals = jnp.where(mine, found, 0.0).astype(BF)
    slot = hot((iota((CAP, SLOTS), 1) & 15) == iota((CAP, SLOTS), 0))
    out_ref[...] = jnp.broadcast_to(mm(slot, vals).astype(BF)[None], (DEVS, CAP, PTS))


def prepare_kernel(pay_ref, links_ref, spread_ref, rows_ref):
    fields, _ = slot_fields(pay_ref)
    tile = (mm_nt(hot((iota((PTS, PTS), 1) >> 4) == F_TILE), fields) + 256.0).astype(I32)
    for k in range(TILES // PTS):
        spread_ref[k * PTS:(k + 1) * PTS, :] = hot(iota((PTS, SLOTS), 0) + k * PTS == tile)
    row, lane = iota((16, PTS), 0), iota((16, PTS), 1) >> 4
    rows = mm_nt(hot((lane == row) & (row < 6)), fields).astype(I32)
    rows_ref[...] = jnp.where(iota((16, SLOTS), 0) == 6, iota((16, SLOTS), 1) >> 4, rows)
    rows_ref[8:10, 0:PTS] = links_ref[...]


def look_up(points, index, source):
    found = jnp.take_along_axis(points, jnp.broadcast_to(index, (PTS, PTS)), axis=1)
    kept = jnp.where((iota((PTS, PTS), 0) >> 2) == source, found, 0.0)
    return jnp.sum(kept.reshape(16, 8, PTS), axis=0)


def post_kernel(me_ref, vals_ref, pay_ref, pos_ref, base_ref, vel_ref, mu_ref, xa_ref, xb_ref,
                za_ref, zb_ref, spread_ref, index_ref, vel_out, moved_out, force_out,
                field_ref, new_ref, points_ref, sems):
    tail = pay_ref[:, 16:24, :].astype(F32).reshape(8 * DEVS, PTS).astype(BF)
    r0, r1 = iota((PTS, 8 * DEVS), 0), iota((PTS, 8 * DEVS), 1)
    same = (r0 >> 2) == (r1 >> 3)
    x_all = mm(hot(same & ((r0 & 3) == (r1 & 3)) & ((r0 & 3) < 3)), tail)
    code = (mm(hot(same & ((r1 & 7) == 3)), tail) + 256.0).astype(I32)
    vals = vals_ref[...].astype(F32).reshape(SLOTS, PTS).T
    vel_all = jnp.zeros((PTS, PTS), F32)
    for k in range(SLOTS // PTS):
        found = jnp.take_along_axis(vals[:, k * PTS:(k + 1) * PTS], code & 127, axis=1)
        vel_all = jnp.where((code >> 7) == k, found, vel_all)
    moved_all = x_all + 0.5 * vel_all
    forces = []
    for k in range(SLOTS // PTS):
        a_low, b_low, own, a_high, b_high, source = [
            index_ref[r:r + 1, k * PTS:(k + 1) * PTS] for r in (F_ALO, F_BLO, F_SELF, F_AHI, F_BHI, 6)
        ]
        ends = look_up(moved_all, a_low, a_high) + look_up(moved_all, b_low, b_high)
        forces.append(ends - 2.0 * look_up(moved_all, own, source))
    force = jnp.concatenate(forces, axis=1)
    hi, mid, lo = split3(force)
    parts = jnp.concatenate([hi.astype(F32), mid.astype(F32), lo.astype(F32)], axis=0).T.astype(BF)
    widen = hot((iota((24, 3 * PTS), 0) & 3) == (iota((24, 3 * PTS), 1) >> 7))
    force = mm(parts, widen)
    w = pay_ref[:, 0:16, :].reshape(SLOTS, PTS).astype(F32)
    for c in range(3):
        part = slice(c * PTS, (c + 1) * PTS)
        field_ref[:, part] = mm(spread_ref[...], (force[:, part] * w).astype(BF))
    me = me_ref[0:1, 0:1]
    own_rows = hot((iota((16, PTS), 1) == me * 4 + iota((16, PTS), 0)) & (iota((16, PTS), 0) < 3))
    moved = pos_ref[...] + 0.5 * mm(own_rows, vel_all.astype(BF))[0:3]
    points_ref[0, 0:3, :] = moved
    ends = jnp.zeros((8, PTS), F32)
    for e in range(2):
        link = index_ref[8 + e:9 + e, 0:PTS]
        ends = ends + look_up(moved_all, link & 127, link >> 7)
    ends = ends[0:4] + ends[4:8]
    points_ref[1, 0:3, :] = ends[0:3] - 2.0 * moved
    copies = [
        pltpu.make_async_copy(points_ref.at[i, pl.ds(0, 3)], out, sems.at[3 + i])
        for i, out in enumerate((moved_out, force_out))
    ]
    for copy in copies:
        copy.start()
    row, lane = iota((16, PTS), 0), iota((16, PTS), 1)
    first, second = pair_ends(me_ref[0:1, 1:2])
    ends = hot(((row == 0) & (lane == first * (PTS - 1))) | ((row == 8) & (lane == second * (PTS - 1))))
    wide_row = iota((16, 512), 0)
    beyond = []
    for c in range(4):
        za, zb = [
            jnp.concatenate([ref[c * 4 + k:c * 4 + k + 1, :].astype(F32) for k in range(4)], axis=1)
            for ref in (za_ref, zb_ref)
        ]
        z = jnp.where(wide_row == 0, za, jnp.where(wide_row == 8, zb, 0.0))
        beyond.append(mm(z.T.astype(BF), ends))
    lane = iota((64, PTS), 1)
    outer = jnp.where((lane == 0) | (lane == PTS - 1), 0.025, 0.0)
    face_z = [outer * (mu_ref[x] + beyond[3][x * 64:x * 64 + 64]) for x in range(8)]
    first, second = [jnp.broadcast_to(end, (64, PTS)) == 1 for end in pair_ends(me)]

    def side(c, x):
        a, b = xa_ref[c].astype(F32), xb_ref[c].astype(F32)
        return jnp.where(first if x else second, a, b)

    face_x = {x: 0.025 * (mu_ref[x] + side(3, x)) for x in (0, 7)}
    for c in range(3):
        for tx in range(2):
            rows = [field_ref[tz * 32 + tx * 16:tz * 32 + tx * 16 + 16, c * PTS:(c + 1) * PTS] for tz in range(16)]
            for xy, part in enumerate(exchange(rows)):
                new_ref[c, 4 * tx + xy // 4, pl.ds(xy % 4, 16, stride=4), :] = part
        for x in range(8):
            beyond_z = beyond[c][x * 64:x * 64 + 64] - vel_ref[c, x]
            new = base_ref[c, x] + 0.05 * new_ref[c, x] + face_z[x] * beyond_z
            if x in face_x:
                new = new + face_x[x] * (side(c, x) - vel_ref[c, x])
            new_ref[c, x] = new
        copies.append(pltpu.make_async_copy(new_ref.at[c], vel_out.at[c], sems.at[c]))
        copies[-1].start()
    for copy in copies:
        copy.wait()


def pair_ends(index):
    first = 1 - (index & 1)
    return first, 1 - first


def faces_kernel(me_ref, vel_ref, mu_ref, xa_ref, xb_ref, za_ref, zb_ref):
    for end, ref in zip(pair_ends(me_ref[0, 0]), (xa_ref, xb_ref)):
        for c in range(3):
            ref[c] = vel_ref[c, end * 7].astype(BF)
        ref[3] = mu_ref[end * 7].astype(BF)
    row, lane = iota((16, PTS), 0), iota((16, PTS), 1)
    first, second = pair_ends(me_ref[0, 1])
    ends = hot(((row < 8) & (lane == first * (PTS - 1))) | ((row >= 8) & (lane == second * (PTS - 1))))
    for c in range(4):
        cells = (vel_ref[c] if c < 3 else mu_ref[...]).reshape(512, PTS).astype(BF)
        found = mm_nt(ends, cells).astype(BF)
        for k in range(4):
            part = slice(k * PTS, (k + 1) * PTS)
            za_ref[c * 4 + k:c * 4 + k + 1, :] = found[0:1, part]
            zb_ref[c * 4 + k:c * 4 + k + 1, :] = found[8:9, part]


def stencil_kernel(vel_ref, mu_ref, out_ref):
    row, lane = iota((64, PTS), 0), iota((64, PTS), 1)

    def plane(c, i):
        return vel_ref[c, i] if c < 3 else mu_ref[i]

    def around(c, x):
        u = plane(c, x)
        out = [
            pltpu.roll(u, 1, 1),
            pltpu.roll(u, PTS - 1, 1),
            jnp.where(row == 0, 0.0, pltpu.roll(u, 1, 0)),
            jnp.where(row == 63, 0.0, pltpu.roll(u, 63, 0)),
        ]
        return u, out + [plane(c, i) for i in (x - 1, x + 1) if 0 <= i < 8]

    inner = [jnp.where(lane == 0, 0.0, 0.025), jnp.where(lane == PTS - 1, 0.0, 0.025)] + [0.025] * 4
    for x in range(8):
        mu, mus = around(3, x)
        faces = [scale * (mu + m) for scale, m in zip(inner, mus)]
        for c in range(3):
            u, us = around(c, x)
            total = u
            for face, other in zip(faces, us):
                total = total + face * (other - u)
            out_ref[c, x] = total


VMEM = pl.BlockSpec(memory_space=pltpu.VMEM)
SMEM = pl.BlockSpec(memory_space=pltpu.SMEM)
HBM = pl.BlockSpec(memory_space=pltpu.HBM)


def call(kernel, outs, scratch, cost, *args, specs=None, out_specs=None):
    return pl.pallas_call(
        kernel,
        out_shape=[jax.ShapeDtypeStruct(s, d) for s, d in outs],
        in_specs=specs or [VMEM] * len(args),
        out_specs=out_specs or [VMEM] * len(outs),
        scratch_shapes=scratch,
        compiler_params=pltpu.CompilerParams(vmem_limit_bytes=16 * 1024 * 1024),
        cost_estimate=pl.CostEstimate(flops=cost * 1000000, bytes_accessed=cost * 4000, transcendentals=0),
    )(*args)


def swap(x, axis, first):
    pairs = []
    for i in range(1 - first, lax.axis_size(axis) - 1, 2):
        pairs += [(i, i + 1), (i + 1, i)]
    return lax.ppermute(x, axis, pairs)


def on_device(velocity, viscosity, positions, weights, tile_index, links):
    me = jnp.stack([lax.axis_index("dev"), lax.axis_index("grp")]).astype(I32).reshape(1, 2)
    links_t = links.T
    (payload,) = call(
        dispatch_kernel, [((DEVS, 24, PTS), BF)],
        [pltpu.VMEM((1, PTS), I32), pltpu.VMEM((2, PTS), I32), pltpu.VMEM((3, PTS), F32), pltpu.VMEM((PTS, PTS), BF),
         pltpu.SemaphoreType.DMA((4,))], 100,
        *[pltpu.with_memory_space_constraint(x, pltpu.HBM)
          for x in (tile_index.reshape(1, PTS), links_t, positions, weights)], specs=[HBM] * 4,
    )
    arrived = lax.all_to_all(payload, "dev", 0, 0, tiled=True)
    xa, xb, za, zb = call(
        faces_kernel, [((4, 64, PTS), BF), ((4, 64, PTS), BF), ((16, PTS), BF), ((16, PTS), BF)], [], 100,
        me, velocity, viscosity, specs=[SMEM, VMEM, VMEM],
    )
    xa = swap(xa, "dev", 1)
    za = swap(za, "grp", 1)
    (tiles,) = call(tiles_kernel, [((TILES, 3 * PTS), BF)], [], 300, velocity)
    (base,) = call(stencil_kernel, [((3, 8, 64, PTS), F32)], [], 500, velocity, viscosity)
    arrived, tiles, base, xa, za, xb, zb = lax.optimization_barrier((arrived, tiles, base, xa, za, xb, zb))
    (values,) = call(velocity_kernel, [((DEVS, CAP, PTS), BF)], [], 500, arrived, tiles)
    all_values = lax.all_to_all(values, "dev", 0, 0, tiled=True)
    xb, zb, arrived, values = lax.optimization_barrier((xb, zb, arrived, values))
    xb = swap(xb, "dev", 0)
    zb = swap(zb, "grp", 0)
    prepared = call(prepare_kernel, [((TILES, SLOTS), BF), ((16, SLOTS), I32)], [], 500, arrived, links_t)
    return call(
        post_kernel, [((3, 8, 64, PTS), F32), ((3, PTS), F32), ((3, PTS), F32)],
        [pltpu.VMEM((TILES, 3 * PTS), F32), pltpu.VMEM((3, 8, 64, PTS), F32), pltpu.VMEM((2, 8, PTS), F32),
         pltpu.SemaphoreType.DMA((5,))], 1000,
        me, all_values, arrived, positions, base, velocity, viscosity, xa, xb, za, zb,
        *prepared, out_specs=[HBM] * 3,
    )


def solution(mesh):
    in_specs = (
        P(None, "dev", None, "grp"),
        P("dev", None, "grp"),
        P(None, ("grp", "dev")),
        P(("grp", "dev"), None),
        P(("grp", "dev")),
        P(("grp", "dev"), None),
    )
    out_specs = (P(None, "dev", None, "grp"), P(None, ("grp", "dev")), P(None, ("grp", "dev")))
    return jax.shard_map(
        lambda *args: tuple(on_device(*args)), mesh=mesh, in_specs=in_specs, out_specs=out_specs, check_vma=False
    )
```

```python
import jax
import jax.numpy as jnp
from jax import lax
from jax.experimental import pallas as pl
from jax.experimental.pallas import tpu as pltpu
from jax.sharding import PartitionSpec as P

F32, BF, I32 = jnp.float32, jnp.bfloat16, jnp.int32
DEVS, CAP, PTS = 32, 16, 128
SLOTS = DEVS * CAP
TILES = 512


def iota(shape, dim):
    return lax.broadcasted_iota(I32, shape, dim)


def hot(cond):
    return jnp.where(cond, 1.0, 0.0).astype(BF)


def mm(a, b):
    return jnp.dot(a, b, preferred_element_type=F32)


def mm_nt(a, b):
    return lax.dot_general(a, b, (((1,), (1,)), ((), ())), preferred_element_type=F32)


def split3(x):
    hi = x.astype(BF)
    rest = x - hi.astype(F32)
    mid = rest.astype(BF)
    return hi, mid, (rest - mid.astype(F32)).astype(BF)


def split2(x):
    hi = x.astype(BF)
    return hi, (x - hi.astype(F32)).astype(BF)


F_TILE, F_SELF, F_ALO, F_AHI, F_BLO, F_BHI = range(6)


def dispatch_kernel(tile_hbm, links_hbm, pos_hbm, w_hbm, out_ref, tile_ref, links_ref, pos_ref, w_ref, sems):
    copies = [
        pltpu.make_async_copy(src, dst, sems.at[i])
        for i, (src, dst) in enumerate(
            ((tile_hbm, tile_ref), (links_hbm, links_ref), (w_hbm, w_ref), (pos_hbm, pos_ref))
        )
    ]
    for copy in copies:
        copy.start()
    for copy in copies:
        copy.wait()
    tile = tile_ref[...]
    owner = tile >> 9
    local = tile & 511
    owned = hot(iota((DEVS, PTS), 0) == owner)
    before = hot(iota((PTS, PTS), 0) < iota((PTS, PTS), 1))
    rank = jnp.sum(owned.astype(F32) * mm(owned, before), axis=0, keepdims=True).astype(I32)
    code = owner * CAP + rank
    place = hot(iota((SLOTS, PTS), 0) == code)
    out_ref[:, 0:16, :] = mm(place, w_ref[...]).astype(BF).reshape(DEVS, CAP, PTS)
    a, b = links_ref[0:1, :], links_ref[1:2, :]
    order = (local & 15) * 32 + (local >> 4) - 256
    fields = [order, iota((1, PTS), 1), a & 127, a >> 7, b & 127, b >> 7] + [jnp.zeros((1, PTS), I32)] * 2
    reps = jnp.concatenate([jnp.broadcast_to(f, (CAP, PTS)) for f in fields], axis=0)
    values = jnp.where((iota((PTS, PTS), 0) & 15) == rank, reps, 0).astype(F32).astype(BF)
    field_rows = mm_nt(owned, values)
    pos = pos_ref[...]
    hi = pos.astype(BF).astype(F32)
    lo = (pos - hi).astype(BF).astype(F32)
    row = iota((8, PTS), 0)
    block = jnp.zeros((8, PTS), F32)
    for c in range(3):
        block = jnp.where(row == c, hi[c:c + 1], block)
        block = jnp.where(row == c + 4, lo[c:c + 1], block)
    block = jnp.where(row == 3, (code - 256).astype(F32), block)
    tail = jnp.where(iota((DEVS, 8, PTS), 1) == 7, field_rows[:, None, :], block[None])
    out_ref[:, 16:24, :] = tail.astype(BF)


def slot_fields(pay_ref):
    block = pay_ref[:, 16:24, :].astype(F32)
    found = jnp.broadcast_to(block[:, 7:8, :], (DEVS, CAP, PTS)).reshape(SLOTS, PTS)
    mine = (iota((SLOTS, PTS), 1) & 15) == (iota((SLOTS, PTS), 0) & 15)
    return jnp.where(mine, found, 0.0).astype(BF), block.reshape(8 * DEVS, PTS).astype(BF)


def exchange(parts):
    group = iota(parts[0].shape, 1) >> 3
    for step in (1, 2, 4, 8):
        odd = (group & step) != 0
        out = list(parts)
        for i in range(16):
            if not i & step:
                j = i | step
                out[i] = jnp.where(odd, pltpu.roll(parts[j], 8 * step, 1), parts[i])
                out[j] = jnp.where(odd, parts[j], pltpu.roll(parts[i], PTS - 8 * step, 1))
        parts = out
    return parts


def tiles_kernel(vel_ref, out_ref):
    for c in range(3):
        for tx in range(2):
            rows = [vel_ref[c, 4 * tx + xy // 4, pl.ds(xy % 4, 16, stride=4), :] for xy in range(16)]
            for tz, part in enumerate(exchange(rows)):
                out_ref[tz * 32 + tx * 16:tz * 32 + tx * 16 + 16, c * PTS:(c + 1) * PTS] = part.astype(BF)


def velocity_kernel(pay_ref, tiles_ref, out_ref):
    rows = jnp.broadcast_to(pay_ref[:, 16:24, :].astype(F32)[:, 7:8, :], (DEVS, CAP, PTS)).reshape(SLOTS, PTS)
    lane = iota((SLOTS, PTS), 1)
    tile = jnp.take_along_axis(rows, F_TILE * CAP + (iota((SLOTS, PTS), 0) & 15), axis=1)
    number = lane.astype(F32) - 256.0
    picks = jnp.concatenate([hot(tile == number + float(k * PTS)) for k in range(TILES // PTS)], axis=1)
    cells = mm(picks, tiles_ref[...])
    w = pay_ref[:, 0:16, :].reshape(SLOTS, PTS).astype(F32)
    hi, lo = split2(cells * jnp.concatenate([w] * 3, axis=1))
    comps = hot((iota((3 * PTS, PTS), 0) >> 7) == (iota((3 * PTS, PTS), 1) & 3))
    found = mm(hi, comps) + mm(lo, comps)
    mine = (lane >> 2) == (iota((SLOTS, PTS), 0) >> 4)
    vals = jnp.where(mine, found, 0.0).astype(BF)
    slot = hot((iota((CAP, SLOTS), 1) & 15) == iota((CAP, SLOTS), 0))
    out_ref[...] = jnp.broadcast_to(mm(slot, vals).astype(BF)[None], (DEVS, CAP, PTS))


def prepare_kernel(pay_ref, links_ref, spread_ref, rows_ref):
    fields, _ = slot_fields(pay_ref)
    tile = (mm_nt(hot((iota((PTS, PTS), 1) >> 4) == F_TILE), fields) + 256.0).astype(I32)
    for k in range(TILES // PTS):
        spread_ref[k * PTS:(k + 1) * PTS, :] = hot(iota((PTS, SLOTS), 0) + k * PTS == tile)
    row, lane = iota((16, PTS), 0), iota((16, PTS), 1) >> 4
    rows = mm_nt(hot((lane == row) & (row < 6)), fields).astype(I32)
    rows_ref[...] = jnp.where(iota((16, SLOTS), 0) == 6, iota((16, SLOTS), 1) >> 4, rows)
    rows_ref[8:10, 0:PTS] = links_ref[...]


def look_up(points, index, source):
    found = jnp.take_along_axis(points, jnp.broadcast_to(index, (PTS, PTS)), axis=1)
    kept = jnp.where((iota((PTS, PTS), 0) >> 2) == source, found, 0.0)
    return jnp.sum(kept.reshape(16, 8, PTS), axis=0)


def post_kernel(me_ref, vals_ref, pay_ref, pos_ref, base_ref, vel_ref, mu_ref, xa_ref, xb_ref,
                za_ref, zb_ref, spread_ref, index_ref, vel_out, moved_out, force_out,
                field_ref, new_ref, points_ref, sems):
    tail = pay_ref[:, 16:24, :].astype(F32).reshape(8 * DEVS, PTS).astype(BF)
    r0, r1 = iota((PTS, 8 * DEVS), 0), iota((PTS, 8 * DEVS), 1)
    same = (r0 >> 2) == (r1 >> 3)
    x_all = mm(hot(same & ((r0 & 3) == (r1 & 3)) & ((r0 & 3) < 3)), tail)
    code = (mm(hot(same & ((r1 & 7) == 3)), tail) + 256.0).astype(I32)
    vals = vals_ref[...].astype(F32).reshape(SLOTS, PTS).T
    vel_all = jnp.zeros((PTS, PTS), F32)
    for k in range(SLOTS // PTS):
        found = jnp.take_along_axis(vals[:, k * PTS:(k + 1) * PTS], code & 127, axis=1)
        vel_all = jnp.where((code >> 7) == k, found, vel_all)
    moved_all = x_all + 0.5 * vel_all
    forces = []
    for k in range(SLOTS // PTS):
        a_low, b_low, own, a_high, b_high, source = [
            index_ref[r:r + 1, k * PTS:(k + 1) * PTS] for r in (F_ALO, F_BLO, F_SELF, F_AHI, F_BHI, 6)
        ]
        ends = look_up(moved_all, a_low, a_high) + look_up(moved_all, b_low, b_high)
        forces.append(ends - 2.0 * look_up(moved_all, own, source))
    force = jnp.concatenate(forces, axis=1)
    hi, mid, lo = split3(force)
    parts = jnp.concatenate([hi.astype(F32), mid.astype(F32), lo.astype(F32)], axis=0).T.astype(BF)
    widen = hot((iota((24, 3 * PTS), 0) & 3) == (iota((24, 3 * PTS), 1) >> 7))
    force = mm(parts, widen)
    w = pay_ref[:, 0:16, :].reshape(SLOTS, PTS).astype(F32)
    for c in range(3):
        part = slice(c * PTS, (c + 1) * PTS)
        field_ref[:, part] = mm(spread_ref[...], (force[:, part] * w).astype(BF))
    me = me_ref[0:1, 0:1]
    own_rows = hot((iota((16, PTS), 1) == me * 4 + iota((16, PTS), 0)) & (iota((16, PTS), 0) < 3))
    moved = pos_ref[...] + 0.5 * mm(own_rows, vel_all.astype(BF))[0:3]
    points_ref[0, 0:3, :] = moved
    ends = jnp.zeros((8, PTS), F32)
    for e in range(2):
        link = index_ref[8 + e:9 + e, 0:PTS]
        ends = ends + look_up(moved_all, link & 127, link >> 7)
    ends = ends[0:4] + ends[4:8]
    points_ref[1, 0:3, :] = ends[0:3] - 2.0 * moved
    copies = [
        pltpu.make_async_copy(points_ref.at[i, pl.ds(0, 3)], out, sems.at[3 + i])
        for i, out in enumerate((moved_out, force_out))
    ]
    for copy in copies:
        copy.start()
    row, lane = iota((16, PTS), 0), iota((16, PTS), 1)
    first, second = pair_ends(me_ref[0:1, 1:2])
    ends = hot(((row == 0) & (lane == first * (PTS - 1))) | ((row == 8) & (lane == second * (PTS - 1))))
    wide_row = iota((16, 512), 0)
    beyond = []
    for c in range(4):
        za, zb = [
            jnp.concatenate([ref[c * 4 + k:c * 4 + k + 1, :].astype(F32) for k in range(4)], axis=1)
            for ref in (za_ref, zb_ref)
        ]
        z = jnp.where(wide_row == 0, za, jnp.where(wide_row == 8, zb, 0.0))
        beyond.append(mm(z.T.astype(BF), ends))
    lane = iota((64, PTS), 1)
    outer = jnp.where((lane == 0) | (lane == PTS - 1), 0.025, 0.0)
    face_z = [outer * (mu_ref[x] + beyond[3][x * 64:x * 64 + 64]) for x in range(8)]
    first, second = [jnp.broadcast_to(end, (64, PTS)) == 1 for end in pair_ends(me)]

    def side(c, x):
        a, b = xa_ref[c].astype(F32), xb_ref[c].astype(F32)
        return jnp.where(first if x else second, a, b)

    face_x = {x: 0.025 * (mu_ref[x] + side(3, x)) for x in (0, 7)}
    for c in range(3):
        for tx in range(2):
            rows = [field_ref[tz * 32 + tx * 16:tz * 32 + tx * 16 + 16, c * PTS:(c + 1) * PTS] for tz in range(16)]
            for xy, part in enumerate(exchange(rows)):
                new_ref[c, 4 * tx + xy // 4, pl.ds(xy % 4, 16, stride=4), :] = part
        for x in range(8):
            beyond_z = beyond[c][x * 64:x * 64 + 64] - vel_ref[c, x]
            new = base_ref[c, x] + 0.05 * new_ref[c, x] + face_z[x] * beyond_z
            if x in face_x:
                new = new + face_x[x] * (side(c, x) - vel_ref[c, x])
            new_ref[c, x] = new
        copies.append(pltpu.make_async_copy(new_ref.at[c], vel_out.at[c], sems.at[c]))
        copies[-1].start()
    for copy in copies:
        copy.wait()


def pair_ends(index):
    first = 1 - (index & 1)
    return first, 1 - first


def faces_kernel(me_ref, vel_ref, mu_ref, xa_ref, xb_ref, za_ref, zb_ref):
    for end, ref in zip(pair_ends(me_ref[0, 0]), (xa_ref, xb_ref)):
        for c in range(3):
            ref[c] = vel_ref[c, end * 7].astype(BF)
        ref[3] = mu_ref[end * 7].astype(BF)
    row, lane = iota((16, PTS), 0), iota((16, PTS), 1)
    first, second = pair_ends(me_ref[0, 1])
    ends = hot(((row < 8) & (lane == first * (PTS - 1))) | ((row >= 8) & (lane == second * (PTS - 1))))
    for c in range(4):
        cells = (vel_ref[c] if c < 3 else mu_ref[...]).reshape(512, PTS).astype(BF)
        found = mm_nt(ends, cells).astype(BF)
        for k in range(4):
            part = slice(k * PTS, (k + 1) * PTS)
            za_ref[c * 4 + k:c * 4 + k + 1, :] = found[0:1, part]
            zb_ref[c * 4 + k:c * 4 + k + 1, :] = found[8:9, part]


def stencil_kernel(vel_ref, mu_ref, out_ref):
    row, lane = iota((64, PTS), 0), iota((64, PTS), 1)

    def plane(c, i):
        return vel_ref[c, i] if c < 3 else mu_ref[i]

    def around(c, x):
        u = plane(c, x)
        out = [
            pltpu.roll(u, 1, 1),
            pltpu.roll(u, PTS - 1, 1),
            jnp.where(row == 0, 0.0, pltpu.roll(u, 1, 0)),
            jnp.where(row == 63, 0.0, pltpu.roll(u, 63, 0)),
        ]
        return u, out + [plane(c, i) for i in (x - 1, x + 1) if 0 <= i < 8]

    inner = [jnp.where(lane == 0, 0.0, 0.025), jnp.where(lane == PTS - 1, 0.0, 0.025)] + [0.025] * 4
    for x in range(8):
        mu, mus = around(3, x)
        faces = [scale * (mu + m) for scale, m in zip(inner, mus)]
        for c in range(3):
            u, us = around(c, x)
            total = u
            for face, other in zip(faces, us):
                total = total + face * (other - u)
            out_ref[c, x] = total


VMEM = pl.BlockSpec(memory_space=pltpu.VMEM)
SMEM = pl.BlockSpec(memory_space=pltpu.SMEM)
HBM = pl.BlockSpec(memory_space=pltpu.HBM)


def call(kernel, outs, scratch, cost, *args, specs=None, out_specs=None):
    return pl.pallas_call(
        kernel,
        out_shape=[jax.ShapeDtypeStruct(s, d) for s, d in outs],
        in_specs=specs or [VMEM] * len(args),
        out_specs=out_specs or [VMEM] * len(outs),
        scratch_shapes=scratch,
        compiler_params=pltpu.CompilerParams(vmem_limit_bytes=16 * 1024 * 1024),
        cost_estimate=pl.CostEstimate(flops=cost * 1000000, bytes_accessed=cost * 4000, transcendentals=0),
    )(*args)


def swap(x, axis, first):
    pairs = []
    for i in range(1 - first, lax.axis_size(axis) - 1, 2):
        pairs += [(i, i + 1), (i + 1, i)]
    return lax.ppermute(x, axis, pairs)


def on_device(velocity, viscosity, positions, weights, tile_index, links):
    me = jnp.stack([lax.axis_index("dev"), lax.axis_index("grp")]).astype(I32).reshape(1, 2)
    links_t = links.T
    (payload,) = call(
        dispatch_kernel, [((DEVS, 24, PTS), BF)],
        [pltpu.VMEM((1, PTS), I32), pltpu.VMEM((2, PTS), I32), pltpu.VMEM((3, PTS), F32), pltpu.VMEM((PTS, PTS), BF),
         pltpu.SemaphoreType.DMA((4,))], 100,
        *[pltpu.with_memory_space_constraint(x, pltpu.HBM)
          for x in (tile_index.reshape(1, PTS), links_t, positions, weights)], specs=[HBM] * 4,
    )
    arrived = lax.all_to_all(payload, "dev", 0, 0, tiled=True)
    xa, xb, za, zb = call(
        faces_kernel, [((4, 64, PTS), BF), ((4, 64, PTS), BF), ((16, PTS), BF), ((16, PTS), BF)], [], 100,
        me, velocity, viscosity, specs=[SMEM, VMEM, VMEM],
    )
    xa = swap(xa, "dev", 1)
    za = swap(za, "grp", 1)
    (tiles,) = call(tiles_kernel, [((TILES, 3 * PTS), BF)], [], 300, velocity)
    (base,) = call(stencil_kernel, [((3, 8, 64, PTS), F32)], [], 500, velocity, viscosity)
    arrived, tiles, base, xa, za, xb, zb = lax.optimization_barrier((arrived, tiles, base, xa, za, xb, zb))
    (values,) = call(velocity_kernel, [((DEVS, CAP, PTS), BF)], [], 500, arrived, tiles)
    all_values = lax.all_to_all(values, "dev", 0, 0, tiled=True)
    xb, zb, arrived, values = lax.optimization_barrier((xb, zb, arrived, values))
    xb = swap(xb, "dev", 0)
    zb = swap(zb, "grp", 0)
    prepared = call(prepare_kernel, [((TILES, SLOTS), BF), ((16, SLOTS), I32)], [], 500, arrived, links_t)
    return call(
        post_kernel, [((3, 8, 64, PTS), F32), ((3, PTS), F32), ((3, PTS), F32)],
        [pltpu.VMEM((TILES, 3 * PTS), F32), pltpu.VMEM((3, 8, 64, PTS), F32), pltpu.VMEM((2, 8, PTS), F32),
         pltpu.SemaphoreType.DMA((5,))], 1000,
        me, all_values, arrived, positions, base, velocity, viscosity, xa, xb, za, zb,
        *prepared, out_specs=[HBM] * 3,
    )


def solution(mesh):
    in_specs = (
        P(None, "dev", None, "grp"),
        P("dev", None, "grp"),
        P(None, ("grp", "dev")),
        P(("grp", "dev"), None),
        P(("grp", "dev")),
        P(("grp", "dev"), None),
    )
    out_specs = (P(None, "dev", None, "grp"), P(None, ("grp", "dev")), P(None, ("grp", "dev")))
    return jax.shard_map(
        lambda *args: tuple(on_device(*args)), mesh=mesh, in_specs=in_specs, out_specs=out_specs, check_vma=False
    )
```

```python
import jax
import jax.numpy as jnp
from jax import lax
from jax.experimental import pallas as pl
from jax.experimental.pallas import tpu as pltpu
from jax.sharding import PartitionSpec as P

F32, BF, I32 = jnp.float32, jnp.bfloat16, jnp.int32
DEVS, CAP, PTS = 32, 16, 128
SLOTS = DEVS * CAP
TILES = 512


def iota(shape, dim):
    return lax.broadcasted_iota(I32, shape, dim)


def hot(cond):
    return jnp.where(cond, 1.0, 0.0).astype(BF)


def mm(a, b):
    return jnp.dot(a, b, preferred_element_type=F32)


def mm_nt(a, b):
    return lax.dot_general(a, b, (((1,), (1,)), ((), ())), preferred_element_type=F32)


def split3(x):
    hi = x.astype(BF)
    rest = x - hi.astype(F32)
    mid = rest.astype(BF)
    return hi, mid, (rest - mid.astype(F32)).astype(BF)


def split2(x):
    hi = x.astype(BF)
    return hi, (x - hi.astype(F32)).astype(BF)


F_TILE, F_SELF, F_ALO, F_AHI, F_BLO, F_BHI = range(6)


def dispatch_kernel(tile_hbm, links_hbm, pos_hbm, w_hbm, out_ref, tile_ref, links_ref, pos_ref, w_ref, sems):
    copies = [
        pltpu.make_async_copy(src, dst, sems.at[i])
        for i, (src, dst) in enumerate(
            ((tile_hbm, tile_ref), (links_hbm, links_ref), (w_hbm, w_ref), (pos_hbm, pos_ref))
        )
    ]
    for copy in copies:
        copy.start()
    for copy in copies:
        copy.wait()
    tile = tile_ref[...]
    owner = tile >> 9
    local = tile & 511
    owned = hot(iota((DEVS, PTS), 0) == owner)
    before = hot(iota((PTS, PTS), 0) < iota((PTS, PTS), 1))
    rank = jnp.sum(owned.astype(F32) * mm(owned, before), axis=0, keepdims=True).astype(I32)
    code = owner * CAP + rank
    place = hot(iota((SLOTS, PTS), 0) == code)
    out_ref[:, 0:16, :] = mm(place, w_ref[...]).astype(BF).reshape(DEVS, CAP, PTS)
    a, b = links_ref[0:1, :], links_ref[1:2, :]
    order = (local & 15) * 32 + (local >> 4) - 256
    fields = [order, iota((1, PTS), 1), a & 127, a >> 7, b & 127, b >> 7] + [jnp.zeros((1, PTS), I32)] * 2
    reps = jnp.concatenate([jnp.broadcast_to(f, (CAP, PTS)) for f in fields], axis=0)
    values = jnp.where((iota((PTS, PTS), 0) & 15) == rank, reps, 0).astype(F32).astype(BF)
    field_rows = mm_nt(owned, values)
    pos = pos_ref[...]
    hi = pos.astype(BF).astype(F32)
    lo = (pos - hi).astype(BF).astype(F32)
    row = iota((8, PTS), 0)
    block = jnp.zeros((8, PTS), F32)
    for c in range(3):
        block = jnp.where(row == c, hi[c:c + 1], block)
        block = jnp.where(row == c + 4, lo[c:c + 1], block)
    block = jnp.where(row == 3, (code - 256).astype(F32), block)
    tail = jnp.where(iota((DEVS, 8, PTS), 1) == 7, field_rows[:, None, :], block[None])
    out_ref[:, 16:24, :] = tail.astype(BF)


def slot_fields(pay_ref):
    block = pay_ref[:, 16:24, :].astype(F32)
    found = jnp.broadcast_to(block[:, 7:8, :], (DEVS, CAP, PTS)).reshape(SLOTS, PTS)
    mine = (iota((SLOTS, PTS), 1) & 15) == (iota((SLOTS, PTS), 0) & 15)
    return jnp.where(mine, found, 0.0).astype(BF), block.reshape(8 * DEVS, PTS).astype(BF)


def exchange(parts):
    group = iota(parts[0].shape, 1) >> 3
    for step in (1, 2, 4, 8):
        odd = (group & step) != 0
        out = list(parts)
        for i in range(16):
            if not i & step:
                j = i | step
                out[i] = jnp.where(odd, pltpu.roll(parts[j], 8 * step, 1), parts[i])
                out[j] = jnp.where(odd, parts[j], pltpu.roll(parts[i], PTS - 8 * step, 1))
        parts = out
    return parts


def tiles_kernel(vel_ref, out_ref):
    for c in range(3):
        for tx in range(2):
            rows = [vel_ref[c, 4 * tx + xy // 4, pl.ds(xy % 4, 16, stride=4), :] for xy in range(16)]
            for tz, part in enumerate(exchange(rows)):
                out_ref[tz * 32 + tx * 16:tz * 32 + tx * 16 + 16, c * PTS:(c + 1) * PTS] = part.astype(BF)


def velocity_kernel(pay_ref, tiles_ref, out_ref):
    rows = jnp.broadcast_to(pay_ref[:, 16:24, :].astype(F32)[:, 7:8, :], (DEVS, CAP, PTS)).reshape(SLOTS, PTS)
    lane = iota((SLOTS, PTS), 1)
    tile = jnp.take_along_axis(rows, F_TILE * CAP + (iota((SLOTS, PTS), 0) & 15), axis=1)
    number = lane.astype(F32) - 256.0
    picks = jnp.concatenate([hot(tile == number + float(k * PTS)) for k in range(TILES // PTS)], axis=1)
    cells = mm(picks, tiles_ref[...])
    w = pay_ref[:, 0:16, :].reshape(SLOTS, PTS).astype(F32)
    hi, lo = split2(cells * jnp.concatenate([w] * 3, axis=1))
    comps = hot((iota((3 * PTS, PTS), 0) >> 7) == (iota((3 * PTS, PTS), 1) & 3))
    found = mm(hi, comps) + mm(lo, comps)
    mine = (lane >> 2) == (iota((SLOTS, PTS), 0) >> 4)
    vals = jnp.where(mine, found, 0.0).astype(BF)
    slot = hot((iota((CAP, SLOTS), 1) & 15) == iota((CAP, SLOTS), 0))
    out_ref[...] = jnp.broadcast_to(mm(slot, vals).astype(BF)[None], (DEVS, CAP, PTS))


def prepare_kernel(pay_ref, links_ref, spread_ref, rows_ref):
    fields, _ = slot_fields(pay_ref)
    tile = (mm_nt(hot((iota((PTS, PTS), 1) >> 4) == F_TILE), fields) + 256.0).astype(I32)
    for k in range(TILES // PTS):
        spread_ref[k * PTS:(k + 1) * PTS, :] = hot(iota((PTS, SLOTS), 0) + k * PTS == tile)
    row, lane = iota((16, PTS), 0), iota((16, PTS), 1) >> 4
    rows = mm_nt(hot((lane == row) & (row < 6)), fields).astype(I32)
    rows_ref[...] = jnp.where(iota((16, SLOTS), 0) == 6, iota((16, SLOTS), 1) >> 4, rows)
    rows_ref[8:10, 0:PTS] = links_ref[...]


def look_up(points, index, source):
    found = jnp.take_along_axis(points, jnp.broadcast_to(index, (PTS, PTS)), axis=1)
    kept = jnp.where((iota((PTS, PTS), 0) >> 2) == source, found, 0.0)
    return jnp.sum(kept.reshape(16, 8, PTS), axis=0)


def post_kernel(me_ref, vals_ref, pay_ref, pos_ref, base_ref, vel_ref, mu_ref, xa_ref, xb_ref,
                za_ref, zb_ref, spread_ref, index_ref, vel_out, moved_out, force_out,
                field_ref, new_ref, points_ref, sems):
    tail = pay_ref[:, 16:24, :].astype(F32).reshape(8 * DEVS, PTS).astype(BF)
    r0, r1 = iota((PTS, 8 * DEVS), 0), iota((PTS, 8 * DEVS), 1)
    same = (r0 >> 2) == (r1 >> 3)
    x_all = mm(hot(same & ((r0 & 3) == (r1 & 3)) & ((r0 & 3) < 3)), tail)
    code = (mm(hot(same & ((r1 & 7) == 3)), tail) + 256.0).astype(I32)
    vals = vals_ref[...].astype(F32).reshape(SLOTS, PTS).T
    vel_all = jnp.zeros((PTS, PTS), F32)
    for k in range(SLOTS // PTS):
        found = jnp.take_along_axis(vals[:, k * PTS:(k + 1) * PTS], code & 127, axis=1)
        vel_all = jnp.where((code >> 7) == k, found, vel_all)
    moved_all = x_all + 0.5 * vel_all
    forces = []
    for k in range(SLOTS // PTS):
        a_low, b_low, own, a_high, b_high, source = [
            index_ref[r:r + 1, k * PTS:(k + 1) * PTS] for r in (F_ALO, F_BLO, F_SELF, F_AHI, F_BHI, 6)
        ]
        ends = look_up(moved_all, a_low, a_high) + look_up(moved_all, b_low, b_high)
        forces.append(ends - 2.0 * look_up(moved_all, own, source))
    force = jnp.concatenate(forces, axis=1)
    hi, mid, lo = split3(force)
    parts = jnp.concatenate([hi.astype(F32), mid.astype(F32), lo.astype(F32)], axis=0).T.astype(BF)
    widen = hot((iota((24, 3 * PTS), 0) & 3) == (iota((24, 3 * PTS), 1) >> 7))
    force = mm(parts, widen)
    w = pay_ref[:, 0:16, :].reshape(SLOTS, PTS).astype(F32)
    me = me_ref[0:1, 0:1]
    own_rows = hot((iota((16, PTS), 1) == me * 4 + iota((16, PTS), 0)) & (iota((16, PTS), 0) < 3))
    moved = pos_ref[...] + 0.5 * mm(own_rows, vel_all.astype(BF))[0:3]
    points_ref[0, 0:3, :] = moved
    ends = jnp.zeros((8, PTS), F32)
    for e in range(2):
        link = index_ref[8 + e:9 + e, 0:PTS]
        ends = ends + look_up(moved_all, link & 127, link >> 7)
    ends = ends[0:4] + ends[4:8]
    points_ref[1, 0:3, :] = ends[0:3] - 2.0 * moved
    copies = [
        pltpu.make_async_copy(points_ref.at[i, pl.ds(0, 3)], out, sems.at[i])
        for i, out in enumerate((moved_out, force_out))
    ]
    for copy in copies:
        copy.start()
    row, lane = iota((16, PTS), 0), iota((16, PTS), 1)
    first, second = pair_ends(me_ref[0:1, 1:2])
    ends = hot(((row == 0) & (lane == first * (PTS - 1))) | ((row == 8) & (lane == second * (PTS - 1))))
    wide_row = iota((16, 512), 0)
    beyond = []
    for c in range(4):
        za, zb = [
            jnp.concatenate([ref[c * 4 + k:c * 4 + k + 1, :].astype(F32) for k in range(4)], axis=1)
            for ref in (za_ref, zb_ref)
        ]
        z = jnp.where(wide_row == 0, za, jnp.where(wide_row == 8, zb, 0.0))
        beyond.append(mm(z.T.astype(BF), ends))
    lane = iota((64, PTS), 1)
    outer = jnp.where((lane == 0) | (lane == PTS - 1), 0.025, 0.0)
    face_z = [outer * (mu_ref[x] + beyond[3][x * 64:x * 64 + 64]) for x in range(8)]
    first, second = [jnp.broadcast_to(end, (64, PTS)) == 1 for end in pair_ends(me)]

    def side(c, x):
        a, b = xa_ref[c].astype(F32), xb_ref[c].astype(F32)
        return jnp.where(first if x else second, a, b)

    face_x = {x: 0.025 * (mu_ref[x] + side(3, x)) for x in (0, 7)}
    for c in range(3):
        part = slice(c * PTS, (c + 1) * PTS)
        field = mm(spread_ref[...], (force[:, part] * w).astype(BF))
        for tx in range(2):
            rows = [field[tz * 32 + tx * 16:tz * 32 + tx * 16 + 16, :] for tz in range(16)]
            for xy, part in enumerate(exchange(rows)):
                new_ref[c, 4 * tx + xy // 4, pl.ds(xy % 4, 16, stride=4), :] = part
            for x in range(4 * tx, 4 * tx + 4):
                beyond_z = beyond[c][x * 64:x * 64 + 64] - vel_ref[c, x]
                new = base_ref[c, x] + 0.05 * new_ref[c, x] + face_z[x] * beyond_z
                if x in face_x:
                    new = new + face_x[x] * (side(c, x) - vel_ref[c, x])
                new_ref[c, x] = new
            part = pl.ds(4 * tx, 4)
            copies.append(pltpu.make_async_copy(new_ref.at[c, part], vel_out.at[c, part], sems.at[2 + 2 * c + tx]))
            copies[-1].start()
    for copy in copies:
        copy.wait()


def pair_ends(index):
    first = 1 - (index & 1)
    return first, 1 - first


def faces_kernel(me_ref, vel_ref, mu_ref, xa_ref, xb_ref, za_ref, zb_ref):
    for end, ref in zip(pair_ends(me_ref[0, 0]), (xa_ref, xb_ref)):
        for c in range(3):
            ref[c] = vel_ref[c, end * 7].astype(BF)
        ref[3] = mu_ref[end * 7].astype(BF)
    row, lane = iota((16, PTS), 0), iota((16, PTS), 1)
    first, second = pair_ends(me_ref[0, 1])
    ends = hot(((row < 8) & (lane == first * (PTS - 1))) | ((row >= 8) & (lane == second * (PTS - 1))))
    for c in range(4):
        cells = (vel_ref[c] if c < 3 else mu_ref[...]).reshape(512, PTS).astype(BF)
        found = mm_nt(ends, cells).astype(BF)
        for k in range(4):
            part = slice(k * PTS, (k + 1) * PTS)
            za_ref[c * 4 + k:c * 4 + k + 1, :] = found[0:1, part]
            zb_ref[c * 4 + k:c * 4 + k + 1, :] = found[8:9, part]


def stencil_kernel(vel_ref, mu_ref, out_ref):
    row, lane = iota((64, PTS), 0), iota((64, PTS), 1)

    def plane(c, i):
        return vel_ref[c, i] if c < 3 else mu_ref[i]

    def around(c, x):
        u = plane(c, x)
        out = [
            pltpu.roll(u, 1, 1),
            pltpu.roll(u, PTS - 1, 1),
            jnp.where(row == 0, 0.0, pltpu.roll(u, 1, 0)),
            jnp.where(row == 63, 0.0, pltpu.roll(u, 63, 0)),
        ]
        return u, out + [plane(c, i) for i in (x - 1, x + 1) if 0 <= i < 8]

    inner = [jnp.where(lane == 0, 0.0, 0.025), jnp.where(lane == PTS - 1, 0.0, 0.025)] + [0.025] * 4
    for x in range(8):
        mu, mus = around(3, x)
        faces = [scale * (mu + m) for scale, m in zip(inner, mus)]
        for c in range(3):
            u, us = around(c, x)
            total = u
            for face, other in zip(faces, us):
                total = total + face * (other - u)
            out_ref[c, x] = total


VMEM = pl.BlockSpec(memory_space=pltpu.VMEM)
SMEM = pl.BlockSpec(memory_space=pltpu.SMEM)
HBM = pl.BlockSpec(memory_space=pltpu.HBM)


def call(kernel, outs, scratch, cost, *args, specs=None, out_specs=None):
    return pl.pallas_call(
        kernel,
        out_shape=[jax.ShapeDtypeStruct(s, d) for s, d in outs],
        in_specs=specs or [VMEM] * len(args),
        out_specs=out_specs or [VMEM] * len(outs),
        scratch_shapes=scratch,
        compiler_params=pltpu.CompilerParams(vmem_limit_bytes=16 * 1024 * 1024),
        cost_estimate=pl.CostEstimate(flops=cost * 1000000, bytes_accessed=cost * 4000, transcendentals=0),
    )(*args)


def swap(x, axis, first):
    pairs = []
    for i in range(1 - first, lax.axis_size(axis) - 1, 2):
        pairs += [(i, i + 1), (i + 1, i)]
    return lax.ppermute(x, axis, pairs)


def on_device(velocity, viscosity, positions, weights, tile_index, links):
    me = jnp.stack([lax.axis_index("dev"), lax.axis_index("grp")]).astype(I32).reshape(1, 2)
    links_t = links.T
    (payload,) = call(
        dispatch_kernel, [((DEVS, 24, PTS), BF)],
        [pltpu.VMEM((1, PTS), I32), pltpu.VMEM((2, PTS), I32), pltpu.VMEM((3, PTS), F32), pltpu.VMEM((PTS, PTS), BF),
         pltpu.SemaphoreType.DMA((4,))], 100,
        *[pltpu.with_memory_space_constraint(x, pltpu.HBM)
          for x in (tile_index.reshape(1, PTS), links_t, positions, weights)], specs=[HBM] * 4,
    )
    arrived = lax.all_to_all(payload, "dev", 0, 0, tiled=True)
    xa, xb, za, zb = call(
        faces_kernel, [((4, 64, PTS), BF), ((4, 64, PTS), BF), ((16, PTS), BF), ((16, PTS), BF)], [], 100,
        me, velocity, viscosity, specs=[SMEM, VMEM, VMEM],
    )
    xa = swap(xa, "dev", 1)
    za = swap(za, "grp", 1)
    (tiles,) = call(tiles_kernel, [((TILES, 3 * PTS), BF)], [], 300, velocity)
    (base,) = call(stencil_kernel, [((3, 8, 64, PTS), F32)], [], 500, velocity, viscosity)
    arrived, tiles, base, xa, za, xb, zb = lax.optimization_barrier((arrived, tiles, base, xa, za, xb, zb))
    (values,) = call(velocity_kernel, [((DEVS, CAP, PTS), BF)], [], 500, arrived, tiles)
    all_values = lax.all_to_all(values, "dev", 0, 0, tiled=True)
    xb, zb, arrived, values = lax.optimization_barrier((xb, zb, arrived, values))
    xb = swap(xb, "dev", 0)
    zb = swap(zb, "grp", 0)
    prepared = call(prepare_kernel, [((TILES, SLOTS), BF), ((16, SLOTS), I32)], [], 500, arrived, links_t)
    return call(
        post_kernel, [((3, 8, 64, PTS), F32), ((3, PTS), F32), ((3, PTS), F32)],
        [pltpu.VMEM((TILES, 3 * PTS), F32), pltpu.VMEM((3, 8, 64, PTS), F32), pltpu.VMEM((2, 8, PTS), F32),
         pltpu.SemaphoreType.DMA((8,))], 1000,
        me, all_values, arrived, positions, base, velocity, viscosity, xa, xb, za, zb,
        *prepared, out_specs=[HBM] * 3,
    )


def solution(mesh):
    in_specs = (
        P(None, "dev", None, "grp"),
        P("dev", None, "grp"),
        P(None, ("grp", "dev")),
        P(("grp", "dev"), None),
        P(("grp", "dev")),
        P(("grp", "dev"), None),
    )
    out_specs = (P(None, "dev", None, "grp"), P(None, ("grp", "dev")), P(None, ("grp", "dev")))
    return jax.shard_map(
        lambda *args: tuple(on_device(*args)), mesh=mesh, in_specs=in_specs, out_specs=out_specs, check_vma=False
    )
```

```python
import jax
import jax.numpy as jnp
from jax import lax
from jax.experimental import pallas as pl
from jax.experimental.pallas import tpu as pltpu
from jax.sharding import PartitionSpec as P

F32, BF, I32 = jnp.float32, jnp.bfloat16, jnp.int32
DEVS, CAP, PTS = 32, 16, 128
SLOTS = DEVS * CAP
TILES = 512


def iota(shape, dim):
    return lax.broadcasted_iota(I32, shape, dim)


def hot(cond):
    return jnp.where(cond, 1.0, 0.0).astype(BF)


def mm(a, b):
    return jnp.dot(a, b, preferred_element_type=F32)


def mm_nt(a, b):
    return lax.dot_general(a, b, (((1,), (1,)), ((), ())), preferred_element_type=F32)


def split3(x):
    hi = x.astype(BF)
    rest = x - hi.astype(F32)
    mid = rest.astype(BF)
    return hi, mid, (rest - mid.astype(F32)).astype(BF)


def split2(x):
    hi = x.astype(BF)
    return hi, (x - hi.astype(F32)).astype(BF)


F_TILE, F_SELF, F_ALO, F_AHI, F_BLO, F_BHI = range(6)


def dispatch_kernel(tile_hbm, links_hbm, pos_hbm, w_hbm, out_ref, tile_ref, links_ref, pos_ref, w_ref, sems):
    copies = [
        pltpu.make_async_copy(src, dst, sems.at[i])
        for i, (src, dst) in enumerate(
            ((tile_hbm, tile_ref), (links_hbm, links_ref), (w_hbm, w_ref), (pos_hbm, pos_ref))
        )
    ]
    for copy in copies:
        copy.start()
    for copy in copies:
        copy.wait()
    tile = tile_ref[...]
    owner = tile >> 9
    local = tile & 511
    owned = hot(iota((DEVS, PTS), 0) == owner)
    before = hot(iota((PTS, PTS), 0) < iota((PTS, PTS), 1))
    rank = jnp.sum(owned.astype(F32) * mm(owned, before), axis=0, keepdims=True).astype(I32)
    code = owner * CAP + rank
    place = hot(iota((SLOTS, PTS), 0) == code)
    out_ref[:, 0:16, :] = mm(place, w_ref[...]).astype(BF).reshape(DEVS, CAP, PTS)
    a, b = links_ref[0:1, :], links_ref[1:2, :]
    order = (local & 15) * 32 + (local >> 4) - 256
    fields = [order, iota((1, PTS), 1), a & 127, a >> 7, b & 127, b >> 7] + [jnp.zeros((1, PTS), I32)] * 2
    reps = jnp.concatenate([jnp.broadcast_to(f, (CAP, PTS)) for f in fields], axis=0)
    values = jnp.where((iota((PTS, PTS), 0) & 15) == rank, reps, 0).astype(F32).astype(BF)
    field_rows = mm_nt(owned, values)
    pos = pos_ref[...]
    hi = pos.astype(BF).astype(F32)
    lo = (pos - hi).astype(BF).astype(F32)
    row = iota((8, PTS), 0)
    block = jnp.zeros((8, PTS), F32)
    for c in range(3):
        block = jnp.where(row == c, hi[c:c + 1], block)
        block = jnp.where(row == c + 4, lo[c:c + 1], block)
    block = jnp.where(row == 3, (code - 256).astype(F32), block)
    tail = jnp.where(iota((DEVS, 8, PTS), 1) == 7, field_rows[:, None, :], block[None])
    out_ref[:, 16:24, :] = tail.astype(BF)


def slot_fields(pay_ref):
    block = pay_ref[:, 16:24, :].astype(F32)
    found = jnp.broadcast_to(block[:, 7:8, :], (DEVS, CAP, PTS)).reshape(SLOTS, PTS)
    mine = (iota((SLOTS, PTS), 1) & 15) == (iota((SLOTS, PTS), 0) & 15)
    return jnp.where(mine, found, 0.0).astype(BF), block.reshape(8 * DEVS, PTS).astype(BF)


def exchange(parts):
    lane = iota(parts[0].shape, 1)
    for step in (8, 4, 2, 1):
        odd = ((lane >> 3) & step) != 0
        other = lane ^ (8 * step)
        out = list(parts)
        for i in range(16):
            if not i & step:
                j = i | step
                moving = jnp.where(odd, parts[i], parts[j])
                moved = pltpu.roll(moving, PTS // 2, 1) if step == 8 else jnp.take_along_axis(moving, other, axis=1)
                out[i] = jnp.where(odd, moved, parts[i])
                out[j] = jnp.where(odd, parts[j], moved)
        parts = out
    return parts


def tiles_kernel(vel_ref, out_ref):
    for c in range(3):
        for tx in range(2):
            rows = [vel_ref[c, 4 * tx + xy // 4, pl.ds(xy % 4, 16, stride=4), :] for xy in range(16)]
            for tz, part in enumerate(exchange(rows)):
                out_ref[tz * 32 + tx * 16:tz * 32 + tx * 16 + 16, c * PTS:(c + 1) * PTS] = part.astype(BF)


def velocity_kernel(pay_ref, tiles_ref, out_ref):
    rows = jnp.broadcast_to(pay_ref[:, 16:24, :].astype(F32)[:, 7:8, :], (DEVS, CAP, PTS)).reshape(SLOTS, PTS)
    lane = iota((SLOTS, PTS), 1)
    tile = jnp.take_along_axis(rows, F_TILE * CAP + (iota((SLOTS, PTS), 0) & 15), axis=1)
    number = lane.astype(F32) - 256.0
    picks = jnp.concatenate([hot(tile == number + float(k * PTS)) for k in range(TILES // PTS)], axis=1)
    cells = mm(picks, tiles_ref[...])
    w = pay_ref[:, 0:16, :].reshape(SLOTS, PTS).astype(F32)
    hi, lo = split2(cells * jnp.concatenate([w] * 3, axis=1))
    comps = hot((iota((3 * PTS, PTS), 0) >> 7) == (iota((3 * PTS, PTS), 1) & 3))
    found = mm(hi, comps) + mm(lo, comps)
    mine = (lane >> 2) == (iota((SLOTS, PTS), 0) >> 4)
    vals = jnp.where(mine, found, 0.0).astype(BF)
    slot = hot((iota((CAP, SLOTS), 1) & 15) == iota((CAP, SLOTS), 0))
    out_ref[...] = jnp.broadcast_to(mm(slot, vals).astype(BF)[None], (DEVS, CAP, PTS))


def prepare_kernel(pay_ref, links_ref, spread_ref, rows_ref):
    fields, _ = slot_fields(pay_ref)
    tile = (mm_nt(hot((iota((PTS, PTS), 1) >> 4) == F_TILE), fields) + 256.0).astype(I32)
    for k in range(TILES // PTS):
        spread_ref[k * PTS:(k + 1) * PTS, :] = hot(iota((PTS, SLOTS), 0) + k * PTS == tile)
    row, lane = iota((16, PTS), 0), iota((16, PTS), 1) >> 4
    rows = mm_nt(hot((lane == row) & (row < 6)), fields).astype(I32)
    rows_ref[...] = jnp.where(iota((16, SLOTS), 0) == 6, iota((16, SLOTS), 1) >> 4, rows)
    rows_ref[8:10, 0:PTS] = links_ref[...]


def look_up(points, index, source):
    found = jnp.take_along_axis(points, jnp.broadcast_to(index, (PTS, PTS)), axis=1)
    kept = jnp.where((iota((PTS, PTS), 0) >> 2) == source, found, 0.0)
    return jnp.sum(kept.reshape(16, 8, PTS), axis=0)


def post_kernel(me_ref, vals_ref, pay_ref, pos_ref, base_ref, vel_ref, mu_ref, xa_ref, xb_ref,
                za_ref, zb_ref, spread_ref, index_ref, vel_out, moved_out, force_out,
                field_ref, new_ref, points_ref, sems):
    tail = pay_ref[:, 16:24, :].astype(F32).reshape(8 * DEVS, PTS).astype(BF)
    r0, r1 = iota((PTS, 8 * DEVS), 0), iota((PTS, 8 * DEVS), 1)
    same = (r0 >> 2) == (r1 >> 3)
    x_all = mm(hot(same & ((r0 & 3) == (r1 & 3)) & ((r0 & 3) < 3)), tail)
    code = (mm(hot(same & ((r1 & 7) == 3)), tail) + 256.0).astype(I32)
    vals = vals_ref[...].astype(F32).reshape(SLOTS, PTS).T
    vel_all = jnp.zeros((PTS, PTS), F32)
    for k in range(SLOTS // PTS):
        found = jnp.take_along_axis(vals[:, k * PTS:(k + 1) * PTS], code & 127, axis=1)
        vel_all = jnp.where((code >> 7) == k, found, vel_all)
    moved_all = x_all + 0.5 * vel_all
    forces = []
    for k in range(SLOTS // PTS):
        a_low, b_low, own, a_high, b_high, source = [
            index_ref[r:r + 1, k * PTS:(k + 1) * PTS] for r in (F_ALO, F_BLO, F_SELF, F_AHI, F_BHI, 6)
        ]
        ends = look_up(moved_all, a_low, a_high) + look_up(moved_all, b_low, b_high)
        forces.append(ends - 2.0 * look_up(moved_all, own, source))
    force = jnp.concatenate(forces, axis=1)
    hi, mid, lo = split3(force)
    parts = jnp.concatenate([hi.astype(F32), mid.astype(F32), lo.astype(F32)], axis=0).T.astype(BF)
    widen = hot((iota((24, 3 * PTS), 0) & 3) == (iota((24, 3 * PTS), 1) >> 7))
    force = mm(parts, widen)
    w = pay_ref[:, 0:16, :].reshape(SLOTS, PTS).astype(F32)
    me = me_ref[0:1, 0:1]
    own_rows = hot((iota((16, PTS), 1) == me * 4 + iota((16, PTS), 0)) & (iota((16, PTS), 0) < 3))
    moved = pos_ref[...] + 0.5 * mm(own_rows, vel_all.astype(BF))[0:3]
    points_ref[0, 0:3, :] = moved
    ends = jnp.zeros((8, PTS), F32)
    for e in range(2):
        link = index_ref[8 + e:9 + e, 0:PTS]
        ends = ends + look_up(moved_all, link & 127, link >> 7)
    ends = ends[0:4] + ends[4:8]
    points_ref[1, 0:3, :] = ends[0:3] - 2.0 * moved
    copies = [
        pltpu.make_async_copy(points_ref.at[i, pl.ds(0, 3)], out, sems.at[i])
        for i, out in enumerate((moved_out, force_out))
    ]
    for copy in copies:
        copy.start()
    row, lane = iota((16, PTS), 0), iota((16, PTS), 1)
    first, second = pair_ends(me_ref[0:1, 1:2])
    ends = hot(((row == 0) & (lane == first * (PTS - 1))) | ((row == 8) & (lane == second * (PTS - 1))))
    wide_row = iota((16, 512), 0)
    beyond = []
    for c in range(4):
        za, zb = [
            jnp.concatenate([ref[c * 4 + k:c * 4 + k + 1, :].astype(F32) for k in range(4)], axis=1)
            for ref in (za_ref, zb_ref)
        ]
        z = jnp.where(wide_row == 0, za, jnp.where(wide_row == 8, zb, 0.0))
        beyond.append(mm(z.T.astype(BF), ends))
    lane = iota((64, PTS), 1)
    outer = jnp.where((lane == 0) | (lane == PTS - 1), 0.025, 0.0)
    face_z = [outer * (mu_ref[x] + beyond[3][x * 64:x * 64 + 64]) for x in range(8)]
    first, second = [jnp.broadcast_to(end, (64, PTS)) == 1 for end in pair_ends(me)]

    def side(c, x):
        a, b = xa_ref[c].astype(F32), xb_ref[c].astype(F32)
        return jnp.where(first if x else second, a, b)

    face_x = {x: 0.025 * (mu_ref[x] + side(3, x)) for x in (0, 7)}
    for c in range(3):
        part = slice(c * PTS, (c + 1) * PTS)
        field = mm(spread_ref[...], (force[:, part] * w).astype(BF))
        for tx in range(2):
            rows = [field[tz * 32 + tx * 16:tz * 32 + tx * 16 + 16, :] for tz in range(16)]
            for xy, part in enumerate(exchange(rows)):
                new_ref[c, 4 * tx + xy // 4, pl.ds(xy % 4, 16, stride=4), :] = part
            for x in range(4 * tx, 4 * tx + 4):
                beyond_z = beyond[c][x * 64:x * 64 + 64] - vel_ref[c, x]
                new = base_ref[c, x] + 0.05 * new_ref[c, x] + face_z[x] * beyond_z
                if x in face_x:
                    new = new + face_x[x] * (side(c, x) - vel_ref[c, x])
                new_ref[c, x] = new
            part = pl.ds(4 * tx, 4)
            copies.append(pltpu.make_async_copy(new_ref.at[c, part], vel_out.at[c, part], sems.at[2 + 2 * c + tx]))
            copies[-1].start()
    for copy in copies:
        copy.wait()


def pair_ends(index):
    first = 1 - (index & 1)
    return first, 1 - first


def faces_kernel(me_ref, vel_ref, mu_ref, xa_ref, xb_ref, za_ref, zb_ref):
    for end, ref in zip(pair_ends(me_ref[0, 0]), (xa_ref, xb_ref)):
        for c in range(3):
            ref[c] = vel_ref[c, end * 7].astype(BF)
        ref[3] = mu_ref[end * 7].astype(BF)
    row, lane = iota((16, PTS), 0), iota((16, PTS), 1)
    first, second = pair_ends(me_ref[0, 1])
    ends = hot(((row < 8) & (lane == first * (PTS - 1))) | ((row >= 8) & (lane == second * (PTS - 1))))
    for c in range(4):
        cells = (vel_ref[c] if c < 3 else mu_ref[...]).reshape(512, PTS).astype(BF)
        found = mm_nt(ends, cells).astype(BF)
        for k in range(4):
            part = slice(k * PTS, (k + 1) * PTS)
            za_ref[c * 4 + k:c * 4 + k + 1, :] = found[0:1, part]
            zb_ref[c * 4 + k:c * 4 + k + 1, :] = found[8:9, part]


def stencil_kernel(vel_ref, mu_ref, out_ref):
    row, lane = iota((64, PTS), 0), iota((64, PTS), 1)

    def plane(c, i):
        return vel_ref[c, i] if c < 3 else mu_ref[i]

    def around(c, x):
        u = plane(c, x)
        out = [
            pltpu.roll(u, 1, 1),
            pltpu.roll(u, PTS - 1, 1),
            jnp.where(row == 0, 0.0, pltpu.roll(u, 1, 0)),
            jnp.where(row == 63, 0.0, pltpu.roll(u, 63, 0)),
        ]
        return u, out + [plane(c, i) for i in (x - 1, x + 1) if 0 <= i < 8]

    inner = [jnp.where(lane == 0, 0.0, 0.025), jnp.where(lane == PTS - 1, 0.0, 0.025)] + [0.025] * 4
    for x in range(8):
        mu, mus = around(3, x)
        faces = [scale * (mu + m) for scale, m in zip(inner, mus)]
        for c in range(3):
            u, us = around(c, x)
            total = u
            for face, other in zip(faces, us):
                total = total + face * (other - u)
            out_ref[c, x] = total


VMEM = pl.BlockSpec(memory_space=pltpu.VMEM)
SMEM = pl.BlockSpec(memory_space=pltpu.SMEM)
HBM = pl.BlockSpec(memory_space=pltpu.HBM)


def call(kernel, outs, scratch, cost, *args, specs=None, out_specs=None):
    return pl.pallas_call(
        kernel,
        out_shape=[jax.ShapeDtypeStruct(s, d) for s, d in outs],
        in_specs=specs or [VMEM] * len(args),
        out_specs=out_specs or [VMEM] * len(outs),
        scratch_shapes=scratch,
        compiler_params=pltpu.CompilerParams(vmem_limit_bytes=16 * 1024 * 1024),
        cost_estimate=pl.CostEstimate(flops=cost * 1000000, bytes_accessed=cost * 4000, transcendentals=0),
    )(*args)


def swap(x, axis, first):
    pairs = []
    for i in range(1 - first, lax.axis_size(axis) - 1, 2):
        pairs += [(i, i + 1), (i + 1, i)]
    return lax.ppermute(x, axis, pairs)


def on_device(velocity, viscosity, positions, weights, tile_index, links):
    me = jnp.stack([lax.axis_index("dev"), lax.axis_index("grp")]).astype(I32).reshape(1, 2)
    links_t = links.T
    (payload,) = call(
        dispatch_kernel, [((DEVS, 24, PTS), BF)],
        [pltpu.VMEM((1, PTS), I32), pltpu.VMEM((2, PTS), I32), pltpu.VMEM((3, PTS), F32), pltpu.VMEM((PTS, PTS), BF),
         pltpu.SemaphoreType.DMA((4,))], 100,
        *[pltpu.with_memory_space_constraint(x, pltpu.HBM)
          for x in (tile_index.reshape(1, PTS), links_t, positions, weights)], specs=[HBM] * 4,
    )
    arrived = lax.all_to_all(payload, "dev", 0, 0, tiled=True)
    xa, xb, za, zb = call(
        faces_kernel, [((4, 64, PTS), BF), ((4, 64, PTS), BF), ((16, PTS), BF), ((16, PTS), BF)], [], 100,
        me, velocity, viscosity, specs=[SMEM, VMEM, VMEM],
    )
    xa = swap(xa, "dev", 1)
    za = swap(za, "grp", 1)
    (tiles,) = call(tiles_kernel, [((TILES, 3 * PTS), BF)], [], 300, velocity)
    (base,) = call(stencil_kernel, [((3, 8, 64, PTS), F32)], [], 500, velocity, viscosity)
    arrived, tiles, base, xa, za, xb, zb = lax.optimization_barrier((arrived, tiles, base, xa, za, xb, zb))
    (values,) = call(velocity_kernel, [((DEVS, CAP, PTS), BF)], [], 500, arrived, tiles)
    all_values = lax.all_to_all(values, "dev", 0, 0, tiled=True)
    xb, zb, arrived, values = lax.optimization_barrier((xb, zb, arrived, values))
    xb = swap(xb, "dev", 0)
    zb = swap(zb, "grp", 0)
    prepared = call(prepare_kernel, [((TILES, SLOTS), BF), ((16, SLOTS), I32)], [], 500, arrived, links_t)
    return call(
        post_kernel, [((3, 8, 64, PTS), F32), ((3, PTS), F32), ((3, PTS), F32)],
        [pltpu.VMEM((TILES, 3 * PTS), F32), pltpu.VMEM((3, 8, 64, PTS), F32), pltpu.VMEM((2, 8, PTS), F32),
         pltpu.SemaphoreType.DMA((8,))], 1000,
        me, all_values, arrived, positions, base, velocity, viscosity, xa, xb, za, zb,
        *prepared, out_specs=[HBM] * 3,
    )


def solution(mesh):
    in_specs = (
        P(None, "dev", None, "grp"),
        P("dev", None, "grp"),
        P(None, ("grp", "dev")),
        P(("grp", "dev"), None),
        P(("grp", "dev")),
        P(("grp", "dev"), None),
    )
    out_specs = (P(None, "dev", None, "grp"), P(None, ("grp", "dev")), P(None, ("grp", "dev")))
    return jax.shard_map(
        lambda *args: tuple(on_device(*args)), mesh=mesh, in_specs=in_specs, out_specs=out_specs, check_vma=False
    )
```

```python
import jax
import jax.numpy as jnp
from jax import lax
from jax.experimental import pallas as pl
from jax.experimental.pallas import tpu as pltpu
from jax.sharding import PartitionSpec as P

F32, BF, I32 = jnp.float32, jnp.bfloat16, jnp.int32
DEVS, CAP, PTS = 32, 16, 128
SLOTS = DEVS * CAP
TILES = 512


def iota(shape, dim):
    return lax.broadcasted_iota(I32, shape, dim)


def hot(cond):
    return jnp.where(cond, 1.0, 0.0).astype(BF)


def mm(a, b):
    return jnp.dot(a, b, preferred_element_type=F32)


def mm_nt(a, b):
    return lax.dot_general(a, b, (((1,), (1,)), ((), ())), preferred_element_type=F32)


def split3(x):
    hi = x.astype(BF)
    rest = x - hi.astype(F32)
    mid = rest.astype(BF)
    return hi, mid, (rest - mid.astype(F32)).astype(BF)


def split2(x):
    hi = x.astype(BF)
    return hi, (x - hi.astype(F32)).astype(BF)


F_TILE, F_SELF, F_ALO, F_AHI, F_BLO, F_BHI = range(6)


def dispatch_kernel(tile_hbm, links_hbm, pos_hbm, w_hbm, out_ref, tile_ref, links_ref, pos_ref, w_ref, sems):
    copies = [
        pltpu.make_async_copy(src, dst, sems.at[i])
        for i, (src, dst) in enumerate(
            ((tile_hbm, tile_ref), (links_hbm, links_ref), (w_hbm, w_ref), (pos_hbm, pos_ref))
        )
    ]
    for copy in copies:
        copy.start()
    for copy in copies:
        copy.wait()
    tile = tile_ref[...]
    owner = tile >> 9
    local = tile & 511
    owned = hot(iota((DEVS, PTS), 0) == owner)
    before = hot(iota((PTS, PTS), 0) < iota((PTS, PTS), 1))
    rank = jnp.sum(owned.astype(F32) * mm(owned, before), axis=0, keepdims=True).astype(I32)
    code = owner * CAP + rank
    place = hot(iota((SLOTS, PTS), 0) == code)
    out_ref[:, 0:16, :] = mm(place, w_ref[...]).astype(BF).reshape(DEVS, CAP, PTS)
    a, b = links_ref[0:1, :], links_ref[1:2, :]
    order = (local & 15) * 32 + (local >> 4) - 256
    fields = [order, iota((1, PTS), 1), a & 127, a >> 7, b & 127, b >> 7] + [jnp.zeros((1, PTS), I32)] * 2
    reps = jnp.concatenate([jnp.broadcast_to(f, (CAP, PTS)) for f in fields], axis=0)
    values = jnp.where((iota((PTS, PTS), 0) & 15) == rank, reps, 0).astype(F32).astype(BF)
    field_rows = mm_nt(owned, values)
    pos = pos_ref[...]
    hi = pos.astype(BF).astype(F32)
    lo = (pos - hi).astype(BF).astype(F32)
    row = iota((8, PTS), 0)
    block = jnp.zeros((8, PTS), F32)
    for c in range(3):
        block = jnp.where(row == c, hi[c:c + 1], block)
        block = jnp.where(row == c + 4, lo[c:c + 1], block)
    block = jnp.where(row == 3, (code - 256).astype(F32), block)
    tail = jnp.where(iota((DEVS, 8, PTS), 1) == 7, field_rows[:, None, :], block[None])
    out_ref[:, 16:24, :] = tail.astype(BF)


def slot_fields(pay_ref):
    block = pay_ref[:, 16:24, :].astype(F32)
    found = jnp.broadcast_to(block[:, 7:8, :], (DEVS, CAP, PTS)).reshape(SLOTS, PTS)
    mine = (iota((SLOTS, PTS), 1) & 15) == (iota((SLOTS, PTS), 0) & 15)
    return jnp.where(mine, found, 0.0).astype(BF), block.reshape(8 * DEVS, PTS).astype(BF)


def exchange(parts):
    lane = iota(parts[0].shape, 1)
    for step in (8, 4, 2, 1):
        odd = ((lane >> 3) & step) != 0
        other = lane ^ (8 * step)
        out = list(parts)
        for i in range(16):
            if not i & step:
                j = i | step
                moving = jnp.where(odd, parts[i], parts[j])
                moved = pltpu.roll(moving, PTS // 2, 1) if step == 8 else jnp.take_along_axis(moving, other, axis=1)
                out[i] = jnp.where(odd, moved, parts[i])
                out[j] = jnp.where(odd, parts[j], moved)
        parts = out
    return parts


def tiles_kernel(vel_ref, out_ref):
    for c in range(3):
        for tx in range(2):
            rows = [vel_ref[c, 4 * tx + xy // 4, pl.ds(xy % 4, 16, stride=4), :] for xy in range(16)]
            for tz, part in enumerate(exchange(rows)):
                out_ref[tz * 32 + tx * 16:tz * 32 + tx * 16 + 16, c * PTS:(c + 1) * PTS] = part.astype(BF)


def velocity_kernel(pay_ref, tiles_ref, out_ref):
    rows = jnp.broadcast_to(pay_ref[:, 16:24, :].astype(F32)[:, 7:8, :], (DEVS, CAP, PTS)).reshape(SLOTS, PTS)
    lane = iota((SLOTS, PTS), 1)
    tile = jnp.take_along_axis(rows, F_TILE * CAP + (iota((SLOTS, PTS), 0) & 15), axis=1)
    number = lane.astype(F32) - 256.0
    picks = jnp.concatenate([hot(tile == number + float(k * PTS)) for k in range(TILES // PTS)], axis=1)
    cells = mm(picks, tiles_ref[...])
    w = pay_ref[:, 0:16, :].reshape(SLOTS, PTS).astype(F32)
    hi, lo = split2(cells * jnp.concatenate([w] * 3, axis=1))
    comps = hot((iota((3 * PTS, PTS), 0) >> 7) == (iota((3 * PTS, PTS), 1) & 3))
    found = mm(hi, comps) + mm(lo, comps)
    mine = (lane >> 2) == (iota((SLOTS, PTS), 0) >> 4)
    vals = jnp.where(mine, found, 0.0).astype(BF)
    slot = hot((iota((CAP, SLOTS), 1) & 15) == iota((CAP, SLOTS), 0))
    out_ref[...] = jnp.broadcast_to(mm(slot, vals).astype(BF)[None], (DEVS, CAP, PTS))


def prepare_kernel(pay_ref, values_ref, links_ref, pos_ref, spread_ref, rows_ref, self_ref):
    fields, tail = slot_fields(pay_ref)
    tile = (mm_nt(hot((iota((PTS, PTS), 1) >> 4) == F_TILE), fields) + 256.0).astype(I32)
    for k in range(TILES // PTS):
        spread_ref[k * PTS:(k + 1) * PTS, :] = hot(iota((PTS, SLOTS), 0) + k * PTS == tile)
    row, lane = iota((16, PTS), 0), iota((16, PTS), 1) >> 4
    rows = mm_nt(hot((lane == row) & (row < 6)), fields).astype(I32)
    rows_ref[...] = rows
    rows_ref[8:10, 0:PTS] = links_ref[...]
    self_ref[8:11, 0:PTS] = pos_ref[...]
    r0, r1 = iota((PTS, 8 * DEVS), 0), iota((PTS, 8 * DEVS), 1)
    x_all = mm(hot(((r0 >> 2) == (r1 >> 3)) & ((r0 & 3) == (r1 & 3)) & ((r0 & 3) < 3)), tail)
    values = jnp.concatenate([values_ref[0].astype(F32)] * 8, axis=0).T
    slot = iota((1, PTS), 1)
    for k in range(SLOTS // PTS):
        part = slice(k * PTS, (k + 1) * PTS)
        source = (slot + k * PTS) >> 4
        here = look_up(x_all, rows[F_SELF:F_SELF + 1, part], source)
        self_ref[0:8, part] = here + 0.5 * look_up(values, slot & 15, source)


def look_up(points, index, source):
    found = jnp.take_along_axis(points, jnp.broadcast_to(index, (PTS, PTS)), axis=1)
    kept = jnp.where((iota((PTS, PTS), 0) >> 2) == source, found, 0.0)
    return jnp.sum(kept.reshape(16, 8, PTS), axis=0)


def post_kernel(me_ref, vals_ref, pay_ref, base_ref, vel_ref, mu_ref, xa_ref, xb_ref,
                za_ref, zb_ref, spread_ref, index_ref, self_ref, vel_out, moved_out, force_out,
                field_ref, new_ref, points_ref, sems):
    tail = pay_ref[:, 16:24, :].astype(F32).reshape(8 * DEVS, PTS).astype(BF)
    r0, r1 = iota((PTS, 8 * DEVS), 0), iota((PTS, 8 * DEVS), 1)
    same = (r0 >> 2) == (r1 >> 3)
    x_all = mm(hot(same & ((r0 & 3) == (r1 & 3)) & ((r0 & 3) < 3)), tail)
    code = (mm(hot(same & ((r1 & 7) == 3)), tail) + 256.0).astype(I32)
    vals = vals_ref[...].astype(F32).reshape(SLOTS, PTS).T
    vel_all = jnp.zeros((PTS, PTS), F32)
    for k in range(SLOTS // PTS):
        found = jnp.take_along_axis(vals[:, k * PTS:(k + 1) * PTS], code & 127, axis=1)
        vel_all = jnp.where((code >> 7) == k, found, vel_all)
    moved_all = x_all + 0.5 * vel_all
    forces = []
    for k in range(SLOTS // PTS):
        part = slice(k * PTS, (k + 1) * PTS)
        a_low, b_low, a_high, b_high = [index_ref[r:r + 1, part] for r in (F_ALO, F_BLO, F_AHI, F_BHI)]
        ends = look_up(moved_all, a_low, a_high) + look_up(moved_all, b_low, b_high)
        forces.append(ends - 2.0 * self_ref[0:8, part])
    force = jnp.concatenate(forces, axis=1)
    hi, mid, lo = split3(force)
    parts = jnp.concatenate([hi.astype(F32), mid.astype(F32), lo.astype(F32)], axis=0).T.astype(BF)
    widen = hot((iota((24, 3 * PTS), 0) & 3) == (iota((24, 3 * PTS), 1) >> 7))
    force = mm(parts, widen)
    w = pay_ref[:, 0:16, :].reshape(SLOTS, PTS).astype(F32)
    me = me_ref[0:1, 0:1]
    own_rows = hot((iota((16, PTS), 1) == me * 4 + iota((16, PTS), 0)) & (iota((16, PTS), 0) < 3))
    moved = self_ref[8:11, 0:PTS] + 0.5 * mm(own_rows, vel_all.astype(BF))[0:3]
    points_ref[0, 0:3, :] = moved
    ends = jnp.zeros((8, PTS), F32)
    for e in range(2):
        link = index_ref[8 + e:9 + e, 0:PTS]
        ends = ends + look_up(moved_all, link & 127, link >> 7)
    ends = ends[0:4] + ends[4:8]
    points_ref[1, 0:3, :] = ends[0:3] - 2.0 * moved
    copies = [
        pltpu.make_async_copy(points_ref.at[i, pl.ds(0, 3)], out, sems.at[i])
        for i, out in enumerate((moved_out, force_out))
    ]
    for copy in copies:
        copy.start()
    row, lane = iota((16, PTS), 0), iota((16, PTS), 1)
    first, second = pair_ends(me_ref[0:1, 1:2])
    ends = hot(((row == 0) & (lane == first * (PTS - 1))) | ((row == 8) & (lane == second * (PTS - 1))))
    wide_row = iota((16, 512), 0)
    beyond = []
    for c in range(4):
        za, zb = [
            jnp.concatenate([ref[c * 4 + k:c * 4 + k + 1, :].astype(F32) for k in range(4)], axis=1)
            for ref in (za_ref, zb_ref)
        ]
        z = jnp.where(wide_row == 0, za, jnp.where(wide_row == 8, zb, 0.0))
        beyond.append(mm(z.T.astype(BF), ends))
    lane = iota((64, PTS), 1)
    outer = jnp.where((lane == 0) | (lane == PTS - 1), 0.025, 0.0)
    face_z = [outer * (mu_ref[x] + beyond[3][x * 64:x * 64 + 64]) for x in range(8)]
    first, second = [jnp.broadcast_to(end, (64, PTS)) == 1 for end in pair_ends(me)]

    def side(c, x):
        a, b = xa_ref[c].astype(F32), xb_ref[c].astype(F32)
        return jnp.where(first if x else second, a, b)

    face_x = {x: 0.025 * (mu_ref[x] + side(3, x)) for x in (0, 7)}
    for c in range(3):
        part = slice(c * PTS, (c + 1) * PTS)
        field = mm(spread_ref[...], (force[:, part] * w).astype(BF))
        for tx in range(2):
            rows = [field[tz * 32 + tx * 16:tz * 32 + tx * 16 + 16, :] for tz in range(16)]
            for xy, part in enumerate(exchange(rows)):
                new_ref[c, 4 * tx + xy // 4, pl.ds(xy % 4, 16, stride=4), :] = part
            for x in range(4 * tx, 4 * tx + 4):
                beyond_z = beyond[c][x * 64:x * 64 + 64] - vel_ref[c, x]
                new = base_ref[c, x] + 0.05 * new_ref[c, x] + face_z[x] * beyond_z
                if x in face_x:
                    new = new + face_x[x] * (side(c, x) - vel_ref[c, x])
                new_ref[c, x] = new
            part = pl.ds(4 * tx, 4)
            copies.append(pltpu.make_async_copy(new_ref.at[c, part], vel_out.at[c, part], sems.at[2 + 2 * c + tx]))
            copies[-1].start()
    for copy in copies:
        copy.wait()


def pair_ends(index):
    first = 1 - (index & 1)
    return first, 1 - first


def faces_kernel(me_ref, vel_ref, mu_ref, xa_ref, xb_ref, za_ref, zb_ref):
    for end, ref in zip(pair_ends(me_ref[0, 0]), (xa_ref, xb_ref)):
        for c in range(3):
            ref[c] = vel_ref[c, end * 7].astype(BF)
        ref[3] = mu_ref[end * 7].astype(BF)
    row, lane = iota((16, PTS), 0), iota((16, PTS), 1)
    first, second = pair_ends(me_ref[0, 1])
    ends = hot(((row < 8) & (lane == first * (PTS - 1))) | ((row >= 8) & (lane == second * (PTS - 1))))
    for c in range(4):
        cells = (vel_ref[c] if c < 3 else mu_ref[...]).reshape(512, PTS).astype(BF)
        found = mm_nt(ends, cells).astype(BF)
        for k in range(4):
            part = slice(k * PTS, (k + 1) * PTS)
            za_ref[c * 4 + k:c * 4 + k + 1, :] = found[0:1, part]
            zb_ref[c * 4 + k:c * 4 + k + 1, :] = found[8:9, part]


def stencil_kernel(vel_ref, mu_ref, out_ref):
    row, lane = iota((64, PTS), 0), iota((64, PTS), 1)

    def plane(c, i):
        return vel_ref[c, i] if c < 3 else mu_ref[i]

    def around(c, x):
        u = plane(c, x)
        out = [
            pltpu.roll(u, 1, 1),
            pltpu.roll(u, PTS - 1, 1),
            jnp.where(row == 0, 0.0, pltpu.roll(u, 1, 0)),
            jnp.where(row == 63, 0.0, pltpu.roll(u, 63, 0)),
        ]
        return u, out + [plane(c, i) for i in (x - 1, x + 1) if 0 <= i < 8]

    inner = [jnp.where(lane == 0, 0.0, 0.025), jnp.where(lane == PTS - 1, 0.0, 0.025)] + [0.025] * 4
    for x in range(8):
        mu, mus = around(3, x)
        faces = [scale * (mu + m) for scale, m in zip(inner, mus)]
        for c in range(3):
            u, us = around(c, x)
            total = u
            for face, other in zip(faces, us):
                total = total + face * (other - u)
            out_ref[c, x] = total


VMEM = pl.BlockSpec(memory_space=pltpu.VMEM)
SMEM = pl.BlockSpec(memory_space=pltpu.SMEM)
HBM = pl.BlockSpec(memory_space=pltpu.HBM)


def call(kernel, outs, scratch, cost, *args, specs=None, out_specs=None):
    return pl.pallas_call(
        kernel,
        out_shape=[jax.ShapeDtypeStruct(s, d) for s, d in outs],
        in_specs=specs or [VMEM] * len(args),
        out_specs=out_specs or [VMEM] * len(outs),
        scratch_shapes=scratch,
        compiler_params=pltpu.CompilerParams(vmem_limit_bytes=16 * 1024 * 1024),
        cost_estimate=pl.CostEstimate(flops=cost * 1000000, bytes_accessed=cost * 4000, transcendentals=0),
    )(*args)


def swap(x, axis, first):
    pairs = []
    for i in range(1 - first, lax.axis_size(axis) - 1, 2):
        pairs += [(i, i + 1), (i + 1, i)]
    return lax.ppermute(x, axis, pairs)


def on_device(velocity, viscosity, positions, weights, tile_index, links):
    me = jnp.stack([lax.axis_index("dev"), lax.axis_index("grp")]).astype(I32).reshape(1, 2)
    links_t = links.T
    (payload,) = call(
        dispatch_kernel, [((DEVS, 24, PTS), BF)],
        [pltpu.VMEM((1, PTS), I32), pltpu.VMEM((2, PTS), I32), pltpu.VMEM((3, PTS), F32), pltpu.VMEM((PTS, PTS), BF),
         pltpu.SemaphoreType.DMA((4,))], 100,
        *[pltpu.with_memory_space_constraint(x, pltpu.HBM)
          for x in (tile_index.reshape(1, PTS), links_t, positions, weights)], specs=[HBM] * 4,
    )
    arrived = lax.all_to_all(payload, "dev", 0, 0, tiled=True)
    xa, xb, za, zb = call(
        faces_kernel, [((4, 64, PTS), BF), ((4, 64, PTS), BF), ((16, PTS), BF), ((16, PTS), BF)], [], 100,
        me, velocity, viscosity, specs=[SMEM, VMEM, VMEM],
    )
    xa = swap(xa, "dev", 1)
    za = swap(za, "grp", 1)
    (tiles,) = call(tiles_kernel, [((TILES, 3 * PTS), BF)], [], 300, velocity)
    (base,) = call(stencil_kernel, [((3, 8, 64, PTS), F32)], [], 500, velocity, viscosity)
    arrived, tiles, base, xa, za, xb, zb = lax.optimization_barrier((arrived, tiles, base, xa, za, xb, zb))
    (values,) = call(velocity_kernel, [((DEVS, CAP, PTS), BF)], [], 500, arrived, tiles)
    all_values = lax.all_to_all(values, "dev", 0, 0, tiled=True)
    xb, zb, arrived, values = lax.optimization_barrier((xb, zb, arrived, values))
    xb = swap(xb, "dev", 0)
    zb = swap(zb, "grp", 0)
    prepared = call(prepare_kernel, [((TILES, SLOTS), BF), ((16, SLOTS), I32), ((16, SLOTS), F32)], [], 500,
        arrived, values, links_t, positions)
    return call(
        post_kernel, [((3, 8, 64, PTS), F32), ((3, PTS), F32), ((3, PTS), F32)],
        [pltpu.VMEM((TILES, 3 * PTS), F32), pltpu.VMEM((3, 8, 64, PTS), F32), pltpu.VMEM((2, 8, PTS), F32),
         pltpu.SemaphoreType.DMA((8,))], 1000,
        me, all_values, arrived, base, velocity, viscosity, xa, xb, za, zb,
        *prepared, out_specs=[HBM] * 3,
    )


def solution(mesh):
    in_specs = (
        P(None, "dev", None, "grp"),
        P("dev", None, "grp"),
        P(None, ("grp", "dev")),
        P(("grp", "dev"), None),
        P(("grp", "dev")),
        P(("grp", "dev"), None),
    )
    out_specs = (P(None, "dev", None, "grp"), P(None, ("grp", "dev")), P(None, ("grp", "dev")))
    return jax.shard_map(
        lambda *args: tuple(on_device(*args)), mesh=mesh, in_specs=in_specs, out_specs=out_specs, check_vma=False
    )
```

```python
import jax
import jax.numpy as jnp
from jax import lax
from jax.experimental import pallas as pl
from jax.experimental.pallas import tpu as pltpu
from jax.sharding import PartitionSpec as P

F32, BF, I32 = jnp.float32, jnp.bfloat16, jnp.int32
DEVS, CAP, PTS = 32, 16, 128
SLOTS = DEVS * CAP
TILES = 512


def iota(shape, dim):
    return lax.broadcasted_iota(I32, shape, dim)


def hot(cond):
    return jnp.where(cond, 1.0, 0.0).astype(BF)


def mm(a, b):
    return jnp.dot(a, b, preferred_element_type=F32)


def mm_nt(a, b):
    return lax.dot_general(a, b, (((1,), (1,)), ((), ())), preferred_element_type=F32)


def split3(x):
    hi = x.astype(BF)
    rest = x - hi.astype(F32)
    mid = rest.astype(BF)
    return hi, mid, (rest - mid.astype(F32)).astype(BF)


def split2(x):
    hi = x.astype(BF)
    return hi, (x - hi.astype(F32)).astype(BF)


F_TILE, F_SELF, F_ALO, F_AHI, F_BLO, F_BHI = range(6)


def dispatch_kernel(tile_hbm, links_hbm, pos_hbm, w_hbm, out_ref, tile_ref, links_ref, pos_ref, w_ref, sems):
    copies = [
        pltpu.make_async_copy(src, dst, sems.at[i])
        for i, (src, dst) in enumerate(
            ((tile_hbm, tile_ref), (links_hbm, links_ref), (w_hbm, w_ref), (pos_hbm, pos_ref))
        )
    ]
    for copy in copies:
        copy.start()
    for copy in copies:
        copy.wait()
    tile = tile_ref[...]
    owner = tile >> 9
    local = tile & 511
    owned = hot(iota((DEVS, PTS), 0) == owner)
    before = hot(iota((PTS, PTS), 0) < iota((PTS, PTS), 1))
    rank = jnp.sum(owned.astype(F32) * mm(owned, before), axis=0, keepdims=True).astype(I32)
    code = owner * CAP + rank
    place = hot(iota((SLOTS, PTS), 0) == code)
    out_ref[:, 0:16, :] = mm(place, w_ref[...]).astype(BF).reshape(DEVS, CAP, PTS)
    a, b = links_ref[0:1, :], links_ref[1:2, :]
    order = (local & 15) * 32 + (local >> 4) - 256
    fields = [order, iota((1, PTS), 1), a & 127, a >> 7, b & 127, b >> 7] + [jnp.zeros((1, PTS), I32)] * 2
    reps = jnp.concatenate([jnp.broadcast_to(f, (CAP, PTS)) for f in fields], axis=0)
    values = jnp.where((iota((PTS, PTS), 0) & 15) == rank, reps, 0).astype(F32).astype(BF)
    field_rows = mm_nt(owned, values)
    pos = pos_ref[...]
    hi = pos.astype(BF).astype(F32)
    lo = (pos - hi).astype(BF).astype(F32)
    row = iota((8, PTS), 0)
    block = jnp.zeros((8, PTS), F32)
    for c in range(3):
        block = jnp.where(row == c, hi[c:c + 1], block)
        block = jnp.where(row == c + 4, lo[c:c + 1], block)
    block = jnp.where(row == 3, (code - 256).astype(F32), block)
    tail = jnp.where(iota((DEVS, 8, PTS), 1) == 7, field_rows[:, None, :], block[None])
    out_ref[:, 16:24, :] = tail.astype(BF)


def slot_fields(pay_ref):
    block = pay_ref[:, 16:24, :].astype(F32)
    found = jnp.broadcast_to(block[:, 7:8, :], (DEVS, CAP, PTS)).reshape(SLOTS, PTS)
    mine = (iota((SLOTS, PTS), 1) & 15) == (iota((SLOTS, PTS), 0) & 15)
    return jnp.where(mine, found, 0.0).astype(BF), block.reshape(8 * DEVS, PTS).astype(BF)


def exchange(parts):
    lane = iota(parts[0].shape, 1)
    for step in (8, 4, 2, 1):
        odd = ((lane >> 3) & step) != 0
        other = lane ^ (8 * step)
        out = list(parts)
        for i in range(16):
            if not i & step:
                j = i | step
                moving = jnp.where(odd, parts[i], parts[j])
                moved = pltpu.roll(moving, PTS // 2, 1) if step == 8 else jnp.take_along_axis(moving, other, axis=1)
                out[i] = jnp.where(odd, moved, parts[i])
                out[j] = jnp.where(odd, parts[j], moved)
        parts = out
    return parts


def tiles_kernel(vel_ref, out_ref):
    for c in range(3):
        for tx in range(2):
            rows = [vel_ref[c, 4 * tx + xy // 4, pl.ds(xy % 4, 16, stride=4), :] for xy in range(16)]
            for tz, part in enumerate(exchange(rows)):
                out_ref[tz * 32 + tx * 16:tz * 32 + tx * 16 + 16, c * PTS:(c + 1) * PTS] = part.astype(BF)


def velocity_kernel(pay_ref, tiles_ref, out_ref):
    rows = jnp.broadcast_to(pay_ref[:, 16:24, :].astype(F32)[:, 7:8, :], (DEVS, CAP, PTS)).reshape(SLOTS, PTS)
    lane = iota((SLOTS, PTS), 1)
    tile = jnp.take_along_axis(rows, F_TILE * CAP + (iota((SLOTS, PTS), 0) & 15), axis=1)
    number = lane.astype(F32) - 256.0
    picks = jnp.concatenate([hot(tile == number + float(k * PTS)) for k in range(TILES // PTS)], axis=1)
    cells = mm(picks, tiles_ref[...])
    w = pay_ref[:, 0:16, :].reshape(SLOTS, PTS).astype(F32)
    hi, lo = split2(cells * jnp.concatenate([w] * 3, axis=1))
    comps = hot((iota((3 * PTS, PTS), 0) >> 7) == (iota((3 * PTS, PTS), 1) & 3))
    found = mm(hi, comps) + mm(lo, comps)
    mine = (lane >> 2) == (iota((SLOTS, PTS), 0) >> 4)
    vals = jnp.where(mine, found, 0.0).astype(BF)
    slot = hot((iota((CAP, SLOTS), 1) & 15) == iota((CAP, SLOTS), 0))
    out_ref[...] = jnp.broadcast_to(mm(slot, vals).astype(BF)[None], (DEVS, CAP, PTS))


def prepare_kernel(pay_ref, values_ref, links_ref, pos_ref, spread_ref, rows_ref, self_ref, group_ref):
    fields, tail = slot_fields(pay_ref)
    tile = (mm_nt(hot((iota((PTS, PTS), 1) >> 4) == F_TILE), fields) + 256.0).astype(I32)
    for k in range(TILES // PTS):
        spread_ref[k * PTS:(k + 1) * PTS, :] = hot(iota((PTS, SLOTS), 0) + k * PTS == tile)
    row, lane = iota((16, PTS), 0), iota((16, PTS), 1) >> 4
    rows = mm_nt(hot((lane == row) & (row < 6)), fields).astype(I32)
    rows_ref[...] = rows
    rows_ref[8:10, 0:PTS] = links_ref[...]
    self_ref[8:11, 0:PTS] = pos_ref[...]
    r0, r1 = iota((PTS, 8 * DEVS), 0), iota((PTS, 8 * DEVS), 1)
    x_all = mm(hot(((r0 >> 2) == (r1 >> 3)) & ((r0 & 3) == (r1 & 3)) & ((r0 & 3) < 3)), tail)
    group_ref[0:PTS, :] = x_all
    group_ref[PTS:, :] = mm(hot(((r0 >> 2) == (r1 >> 3)) & ((r1 & 7) == 3)), tail) + 256.0
    values = jnp.concatenate([values_ref[0].astype(F32)] * 8, axis=0).T
    slot = iota((1, PTS), 1)
    for k in range(SLOTS // PTS):
        part = slice(k * PTS, (k + 1) * PTS)
        source = (slot + k * PTS) >> 4
        here = look_up(x_all, rows[F_SELF:F_SELF + 1, part], source)
        self_ref[0:8, part] = here + 0.5 * look_up(values, slot & 15, source)


def look_up(points, index, source):
    found = jnp.take_along_axis(points, jnp.broadcast_to(index, (PTS, PTS)), axis=1)
    kept = jnp.where((iota((PTS, PTS), 0) >> 2) == source, found, 0.0)
    return jnp.sum(kept.reshape(16, 8, PTS), axis=0)


def post_kernel(me_ref, vals_ref, pay_ref, base_ref, vel_ref, mu_ref, xa_ref, xb_ref,
                za_ref, zb_ref, spread_ref, index_ref, self_ref, group_ref, vel_out, moved_out, force_out,
                field_ref, new_ref, points_ref, sems):
    code = group_ref[PTS:, :].astype(I32)
    vals = vals_ref[...].astype(F32).reshape(SLOTS, PTS).T
    vel_all = jnp.zeros((PTS, PTS), F32)
    for k in range(SLOTS // PTS):
        found = jnp.take_along_axis(vals[:, k * PTS:(k + 1) * PTS], code & 127, axis=1)
        vel_all = jnp.where((code >> 7) == k, found, vel_all)
    moved_all = group_ref[0:PTS, :] + 0.5 * vel_all
    forces = []
    for k in range(SLOTS // PTS):
        part = slice(k * PTS, (k + 1) * PTS)
        a_low, b_low, a_high, b_high = [index_ref[r:r + 1, part] for r in (F_ALO, F_BLO, F_AHI, F_BHI)]
        ends = look_up(moved_all, a_low, a_high) + look_up(moved_all, b_low, b_high)
        forces.append(ends - 2.0 * self_ref[0:8, part])
    force = jnp.concatenate(forces, axis=1)
    hi, mid, lo = split3(force)
    parts = jnp.concatenate([hi.astype(F32), mid.astype(F32), lo.astype(F32)], axis=0).T.astype(BF)
    widen = hot((iota((24, 3 * PTS), 0) & 3) == (iota((24, 3 * PTS), 1) >> 7))
    force = mm(parts, widen)
    w = pay_ref[:, 0:16, :].reshape(SLOTS, PTS).astype(F32)
    me = me_ref[0:1, 0:1]
    own_rows = hot((iota((16, PTS), 1) == me * 4 + iota((16, PTS), 0)) & (iota((16, PTS), 0) < 3))
    moved = self_ref[8:11, 0:PTS] + 0.5 * mm(own_rows, vel_all.astype(BF))[0:3]
    points_ref[0, 0:3, :] = moved
    ends = jnp.zeros((8, PTS), F32)
    for e in range(2):
        link = index_ref[8 + e:9 + e, 0:PTS]
        ends = ends + look_up(moved_all, link & 127, link >> 7)
    ends = ends[0:4] + ends[4:8]
    points_ref[1, 0:3, :] = ends[0:3] - 2.0 * moved
    copies = [
        pltpu.make_async_copy(points_ref.at[i, pl.ds(0, 3)], out, sems.at[i])
        for i, out in enumerate((moved_out, force_out))
    ]
    for copy in copies:
        copy.start()
    row, lane = iota((16, PTS), 0), iota((16, PTS), 1)
    first, second = pair_ends(me_ref[0:1, 1:2])
    ends = hot(((row == 0) & (lane == first * (PTS - 1))) | ((row == 8) & (lane == second * (PTS - 1))))
    wide_row = iota((16, 512), 0)
    beyond = []
    for c in range(4):
        za, zb = [
            jnp.concatenate([ref[c * 4 + k:c * 4 + k + 1, :].astype(F32) for k in range(4)], axis=1)
            for ref in (za_ref, zb_ref)
        ]
        z = jnp.where(wide_row == 0, za, jnp.where(wide_row == 8, zb, 0.0))
        beyond.append(mm(z.T.astype(BF), ends))
    lane = iota((64, PTS), 1)
    outer = jnp.where((lane == 0) | (lane == PTS - 1), 0.025, 0.0)
    face_z = [outer * (mu_ref[x] + beyond[3][x * 64:x * 64 + 64]) for x in range(8)]
    first, second = [jnp.broadcast_to(end, (64, PTS)) == 1 for end in pair_ends(me)]

    def side(c, x):
        a, b = xa_ref[c].astype(F32), xb_ref[c].astype(F32)
        return jnp.where(first if x else second, a, b)

    face_x = {x: 0.025 * (mu_ref[x] + side(3, x)) for x in (0, 7)}
    for c in range(3):
        part = slice(c * PTS, (c + 1) * PTS)
        field = mm(spread_ref[...], (force[:, part] * w).astype(BF))
        for tx in range(2):
            rows = [field[tz * 32 + tx * 16:tz * 32 + tx * 16 + 16, :] for tz in range(16)]
            for xy, part in enumerate(exchange(rows)):
                new_ref[c, 4 * tx + xy // 4, pl.ds(xy % 4, 16, stride=4), :] = part
            for x in range(4 * tx, 4 * tx + 4):
                beyond_z = beyond[c][x * 64:x * 64 + 64] - vel_ref[c, x]
                new = base_ref[c, x] + 0.05 * new_ref[c, x] + face_z[x] * beyond_z
                if x in face_x:
                    new = new + face_x[x] * (side(c, x) - vel_ref[c, x])
                new_ref[c, x] = new
            part = pl.ds(4 * tx, 4)
            copies.append(pltpu.make_async_copy(new_ref.at[c, part], vel_out.at[c, part], sems.at[2 + 2 * c + tx]))
            copies[-1].start()
    for copy in copies:
        copy.wait()


def pair_ends(index):
    first = 1 - (index & 1)
    return first, 1 - first


def faces_kernel(me_ref, vel_ref, mu_ref, xa_ref, xb_ref, za_ref, zb_ref):
    for end, ref in zip(pair_ends(me_ref[0, 0]), (xa_ref, xb_ref)):
        for c in range(3):
            ref[c] = vel_ref[c, end * 7].astype(BF)
        ref[3] = mu_ref[end * 7].astype(BF)
    row, lane = iota((16, PTS), 0), iota((16, PTS), 1)
    first, second = pair_ends(me_ref[0, 1])
    ends = hot(((row < 8) & (lane == first * (PTS - 1))) | ((row >= 8) & (lane == second * (PTS - 1))))
    for c in range(4):
        cells = (vel_ref[c] if c < 3 else mu_ref[...]).reshape(512, PTS).astype(BF)
        found = mm_nt(ends, cells).astype(BF)
        for k in range(4):
            part = slice(k * PTS, (k + 1) * PTS)
            za_ref[c * 4 + k:c * 4 + k + 1, :] = found[0:1, part]
            zb_ref[c * 4 + k:c * 4 + k + 1, :] = found[8:9, part]


def stencil_kernel(vel_ref, mu_ref, out_ref):
    row, lane = iota((64, PTS), 0), iota((64, PTS), 1)

    def plane(c, i):
        return vel_ref[c, i] if c < 3 else mu_ref[i]

    def around(c, x):
        u = plane(c, x)
        out = [
            pltpu.roll(u, 1, 1),
            pltpu.roll(u, PTS - 1, 1),
            jnp.where(row == 0, 0.0, pltpu.roll(u, 1, 0)),
            jnp.where(row == 63, 0.0, pltpu.roll(u, 63, 0)),
        ]
        return u, out + [plane(c, i) for i in (x - 1, x + 1) if 0 <= i < 8]

    inner = [jnp.where(lane == 0, 0.0, 0.025), jnp.where(lane == PTS - 1, 0.0, 0.025)] + [0.025] * 4
    for x in range(8):
        mu, mus = around(3, x)
        faces = [scale * (mu + m) for scale, m in zip(inner, mus)]
        for c in range(3):
            u, us = around(c, x)
            total = u
            for face, other in zip(faces, us):
                total = total + face * (other - u)
            out_ref[c, x] = total


VMEM = pl.BlockSpec(memory_space=pltpu.VMEM)
SMEM = pl.BlockSpec(memory_space=pltpu.SMEM)
HBM = pl.BlockSpec(memory_space=pltpu.HBM)


def call(kernel, outs, scratch, cost, *args, specs=None, out_specs=None):
    return pl.pallas_call(
        kernel,
        out_shape=[jax.ShapeDtypeStruct(s, d) for s, d in outs],
        in_specs=specs or [VMEM] * len(args),
        out_specs=out_specs or [VMEM] * len(outs),
        scratch_shapes=scratch,
        compiler_params=pltpu.CompilerParams(vmem_limit_bytes=16 * 1024 * 1024),
        cost_estimate=pl.CostEstimate(flops=cost * 1000000, bytes_accessed=cost * 4000, transcendentals=0),
    )(*args)


def swap(x, axis, first):
    pairs = []
    for i in range(1 - first, lax.axis_size(axis) - 1, 2):
        pairs += [(i, i + 1), (i + 1, i)]
    return lax.ppermute(x, axis, pairs)


def on_device(velocity, viscosity, positions, weights, tile_index, links):
    me = jnp.stack([lax.axis_index("dev"), lax.axis_index("grp")]).astype(I32).reshape(1, 2)
    links_t = links.T
    (payload,) = call(
        dispatch_kernel, [((DEVS, 24, PTS), BF)],
        [pltpu.VMEM((1, PTS), I32), pltpu.VMEM((2, PTS), I32), pltpu.VMEM((3, PTS), F32), pltpu.VMEM((PTS, PTS), BF),
         pltpu.SemaphoreType.DMA((4,))], 100,
        *[pltpu.with_memory_space_constraint(x, pltpu.HBM)
          for x in (tile_index.reshape(1, PTS), links_t, positions, weights)], specs=[HBM] * 4,
    )
    arrived = lax.all_to_all(payload, "dev", 0, 0, tiled=True)
    xa, xb, za, zb = call(
        faces_kernel, [((4, 64, PTS), BF), ((4, 64, PTS), BF), ((16, PTS), BF), ((16, PTS), BF)], [], 100,
        me, velocity, viscosity, specs=[SMEM, VMEM, VMEM],
    )
    xa = swap(xa, "dev", 1)
    za = swap(za, "grp", 1)
    (tiles,) = call(tiles_kernel, [((TILES, 3 * PTS), BF)], [], 300, velocity)
    (base,) = call(stencil_kernel, [((3, 8, 64, PTS), F32)], [], 500, velocity, viscosity)
    arrived, tiles, base, xa, za, xb, zb = lax.optimization_barrier((arrived, tiles, base, xa, za, xb, zb))
    (values,) = call(velocity_kernel, [((DEVS, CAP, PTS), BF)], [], 500, arrived, tiles)
    all_values = lax.all_to_all(values, "dev", 0, 0, tiled=True)
    xb, zb, arrived, values = lax.optimization_barrier((xb, zb, arrived, values))
    xb = swap(xb, "dev", 0)
    zb = swap(zb, "grp", 0)
    prepared = call(prepare_kernel, [((TILES, SLOTS), BF), ((16, SLOTS), I32), ((16, SLOTS), F32),
         ((2 * PTS, PTS), F32)], [], 500,
        arrived, values, links_t, positions)
    return call(
        post_kernel, [((3, 8, 64, PTS), F32), ((3, PTS), F32), ((3, PTS), F32)],
        [pltpu.VMEM((TILES, 3 * PTS), F32), pltpu.VMEM((3, 8, 64, PTS), F32), pltpu.VMEM((2, 8, PTS), F32),
         pltpu.SemaphoreType.DMA((8,))], 1000,
        me, all_values, arrived, base, velocity, viscosity, xa, xb, za, zb,
        *prepared, out_specs=[HBM] * 3,
    )


def solution(mesh):
    in_specs = (
        P(None, "dev", None, "grp"),
        P("dev", None, "grp"),
        P(None, ("grp", "dev")),
        P(("grp", "dev"), None),
        P(("grp", "dev")),
        P(("grp", "dev"), None),
    )
    out_specs = (P(None, "dev", None, "grp"), P(None, ("grp", "dev")), P(None, ("grp", "dev")))
    return jax.shard_map(
        lambda *args: tuple(on_device(*args)), mesh=mesh, in_specs=in_specs, out_specs=out_specs, check_vma=False
    )
```
